128 devices in a mesh: doc: 4 (over z_lo, core), param: 32 (over x, z_hi, y).
Axes of the slice: x: 4, y: 4, z: 4 (z_hi: 2, z_lo: 2; z = z_hi * 2 + z_lo), core: 2. Of those that a mesh axis runs over, the one named last changes fastest.
Arguments:
- layer_input: bfloat16 [2048, 8192], P('doc', 'param'), may hold values from -6 to 6
- output_grad: bfloat16 [2048, 8192], P('doc', 'param'), may hold values from -0.29882812 to 0.29882812
- doc_ids: int32 [2048], P('doc'), may hold values from 0 to 3, never falling along the last dimension, each value on 1 to 1536 neighbouring positions
- sign_bits: int32 [8192, 8192], P('param'), may hold values from 0 to 1
- kept_rows: int32 [8192], replicated, may hold values from 0 to 8191
- kept_cols: int32 [8192], replicated, may hold values from 0 to 8191
Outputs:
- sketch: float32 [4, 8192], P('doc', 'param')
The draws below stay inside these ranges and needn't reach their ends.
Inputs may be any that keep to these rules, and one draw needn't show every extreme that they name: `doc_ids`: document numbers never fall along the packed rows; every document has 1 to 1536 rows and one has exactly 1536.
All inputs are finite; a program needn't handle non-finite values.
Results may differ from the reference program's by a relative error of at most 0.0003.
Values may be sent and summed in bfloat16 or wider, within the bound.
A program may use at most 128 MiB of HBM per device.

```python
import math
import jax
import jax.numpy as jnp
import numpy as np
from jax import lax

D = 8192
K = 8192
DOCS = 4
TOKENS = 2048
MOST = 1536


def set_ends(entries, key, least, largest):
    longest = entries.shape.index(max(entries.shape))
    spots = []
    for shift in (0, 1):
        where = [jax.random.randint(jax.random.fold_in(key, axis), (), 0, length) for axis, length in enumerate(entries.shape)]
        where[longest] = (where[longest] + shift) % entries.shape[longest]
        spots.append(tuple(where))
    return entries.at[spots[0]].set(least).at[spots[1]].set(largest)


def block_scale(stream_key, dims, pieces, smallest, largest):
    def one(dim, blocks):
        heights = jax.random.uniform(jax.random.fold_in(jax.random.fold_in(stream_key, 6), dim), (blocks,), jnp.float32, smallest / len(pieces), largest / len(pieces))
        return jnp.repeat(jnp.exp(heights), dims[dim] // blocks).reshape((-1,) + (1,) * (len(dims) - dim - 1))

    factor_of = one(*pieces[0])
    for cut in pieces[1:]:
        factor_of = factor_of * one(*cut)
    return factor_of


def split_up(number_of, total, reach, lean):
    weights = [(1 << 20) // math.isqrt(rank ** lean) + 1 for rank in range(2, number_of + 1)]
    surplus, counts = total - reach - (number_of - 1), [1] * (number_of - 1)
    while surplus > 0:
        candidates = [i for i in range(number_of - 1) if counts[i] < reach]
        mass, budget = sum([weights[i] for i in candidates]), surplus
        for i in candidates:
            extra = min(reach - counts[i], max(1, budget * weights[i] // mass), surplus)
            counts[i] = counts[i] + extra
            surplus = surplus - extra
    return np.array([reach] + counts)


def uneven(stream_key, number_of, total, limit, skew):
    if number_of == 2:
        one = jax.random.randint(stream_key, (), max(1, total - limit), min(limit, total - 1) + 1)
        return jnp.stack([one, total - one])
    lengths = jnp.asarray(split_up(number_of, total, limit, skew), jnp.int32)
    couples = (number_of - 1) // 2
    donor, receiver = lengths[1:1 + 2 * couples:2], lengths[2:2 + 2 * couples:2]
    margin = jnp.minimum(donor - 1, limit - receiver)
    moved = jax.random.randint(jax.random.fold_in(stream_key, 1), (couples,), 0, 1 << 20) % (margin + 1)
    lengths = lengths.at[1:1 + 2 * couples:2].set(donor - moved).at[2:2 + 2 * couples:2].set(receiver + moved)
    return lengths[jax.random.permutation(jax.random.fold_in(stream_key, 2), number_of)]


def gaussian(own_key, shape, spread, bound, pieces=(), held_as=jnp.bfloat16):
    level = block_scale(own_key, shape, pieces, -0.22, 0.18) if pieces else 1.0
    entries = jax.random.normal(own_key, shape, jnp.float32) * spread * level
    return jnp.minimum(jnp.maximum(entries, -bound), bound).astype(held_as)


def setup_inputs(seed: int = 0) -> dict:
    keys = jax.random.split(jax.random.key(seed), 7)
    layer_input = gaussian(keys[0], (TOKENS, D), 1.0, 6.0, ((0, 4), (1, 32)))
    output_grad = gaussian(keys[1], (TOKENS, D), 0.05, 0.29882812, ((0, 4), (1, 32)))
    doc_ids = jnp.searchsorted(jnp.cumsum(uneven(keys[2], DOCS, TOKENS, MOST, 2)), jnp.arange(TOKENS), side="right").astype(jnp.int32)
    sign_bits = set_ends(jax.random.randint(keys[3], (D, D), 0, 2), jax.random.fold_in(keys[3], 1), 0, 1).astype(jnp.int32)
    kept_rows = set_ends(jax.random.randint(keys[4], (K,), 0, D), jax.random.fold_in(keys[4], 1), 0, D - 1).astype(jnp.int32)
    kept_cols = set_ends(jax.random.randint(keys[5], (K,), 0, D), jax.random.fold_in(keys[5], 1), 0, D - 1).astype(jnp.int32)
    return dict(layer_input=layer_input, output_grad=output_grad, doc_ids=doc_ids, sign_bits=sign_bits, kept_rows=kept_rows, kept_cols=kept_cols)


def sign_table(size):
    index = jnp.arange(size, dtype=jnp.int32)
    common = index[:, None] & index[None, :]
    count = jnp.zeros((size, size), jnp.int32)
    for bit in range(max(size.bit_length() - 1, 1)):
        count = count + ((common >> bit) & 1)
    return (1 - 2 * (count % 2)).astype(jnp.float32)


def hadamard(block3, length):
    lead, middle, tail = block3.shape
    done = 1
    while done < length:
        factor = min(128, length // done)
        view = block3.reshape(lead * done, factor, (length // (done * factor)) * tail)
        view = jnp.einsum("afb,gf->agb", view, sign_table(factor), precision=lax.Precision.HIGHEST)
        block3 = view.reshape(lead, length, tail)
        done = done * factor
    return block3


def reference(layer_input, output_grad, doc_ids, sign_bits, kept_rows, kept_cols):
    signs = (2 * sign_bits - 1).astype(jnp.float32)
    spare = jnp.zeros((MOST, D), layer_input.dtype)
    padded_in = jnp.concatenate([layer_input, spare], axis=0)
    padded_grad = jnp.concatenate([output_grad, spare], axis=0)
    offsets = jnp.arange(MOST, dtype=jnp.int32)
    results = []
    for label in range(DOCS):
        start = jnp.sum((doc_ids < label).astype(jnp.int32)).astype(jnp.int32)
        length = jnp.sum((doc_ids == label).astype(jnp.int32))
        live = (offsets < length)[:, None]
        take_in = jnp.where(live, lax.dynamic_slice_in_dim(padded_in, start, MOST, 0), 0).astype(layer_input.dtype)
        take_grad = jnp.where(live, lax.dynamic_slice_in_dim(padded_grad, start, MOST, 0), 0).astype(output_grad.dtype)
        gradient = lax.dot_general(take_in, take_grad, (((0,), (0,)), ((), ())), preferred_element_type=jnp.float32)
        mixed = hadamard((gradient * signs).reshape(1, D, D), D)
        mixed = hadamard(mixed.reshape(D, D, 1), D).reshape(D, D)
        results.append(mixed[kept_rows, kept_cols] / D)
    return jnp.stack(results)
```

```python
import functools

import jax
import jax.numpy as jnp
from jax import lax
from jax.experimental import pallas as pl
from jax.experimental.pallas import tpu as pltpu
from jax.sharding import PartitionSpec as P

MESH = pl.DeviceIdType.MESH
F32, BF16, I32 = jnp.float32, jnp.bfloat16, jnp.int32

WAITS = [
    [(0, 1, 0), (0, 3, 0), (1, 0, 1), (1, 0, 3)],
    [(0, 0, 1), (0, 0, 3), (1, 1, 0), (1, 3, 0)],
    [(0, 2, 0), (1, 0, 2)],
    [(0, 1, 1), (1, 1, 1), (0, 1, 3), (1, 3, 1), (0, 3, 1), (1, 1, 3), (0, 3, 3), (1, 3, 3)],
    [(0, 0, 2), (1, 2, 0)],
    [(0, 2, 1), (1, 1, 2), (0, 2, 3), (1, 3, 2)],
    [(0, 1, 2), (1, 2, 1), (0, 3, 2), (1, 2, 3)],
    [(0, 2, 2), (1, 2, 2)],
]
PAIRS = [
    [],
    [],
    [((1, 0), (3, 0))],
    [((0, 1), (0, 3))],
    [((0, 0), (2, 0)), ((1, 1), (3, 3))],
    [((1, 3), (3, 1))],
    [((2, 1), (2, 3)), ((1, 2), (3, 2))],
    [((0, 2), (2, 2))],
]


def hops(piece, u, v):
    a, b = (u, v) if piece == 0 else (v, u)
    if (a, b) == (0, 0):
        out = [(1, 0), (3, 0), (0, 1), (0, 3)]
    elif b == 0:
        out = ([(1, 0)] if a == 1 else []) + [(0, 1), (0, 3)]
    elif b == 1:
        out = [(0, 1)]
    else:
        out = []
    return out if piece == 0 else [(d, c) for c, d in out]


def parity(t):
    for s in (8, 4, 2, 1):
        t = t ^ (t >> s)
    return t & 1


def sylvester(n):
    i = lax.broadcasted_iota(I32, (n, n), 0)
    j = lax.broadcasted_iota(I32, (n, n), 1)
    return (1 - 2 * parity(i & j)).astype(F32).astype(BF16)


def halves(t):
    hi = t.astype(BF16)
    lo = (t - hi.astype(F32)).astype(BF16)
    return hi, lo


def kernel(
    li, og, ids, sb, kr, kc, out,
    gbuf, zb, z2, xq, xtb, xto, sg, stl, sts, sgs, idall, hm, lane_v, base_v, sgn_v, base_s,
    sa0, sa1, sa2, sa3, ps, pd, r1, q2, r2,
    gs, gr, ss, sr, xs_, xr, xl, ds_, dr, ls, lt, sgss, sgr, km, s1, w1, s2, w2,
):
    d = lax.axis_index("doc")
    p = lax.axis_index("param")
    x, zh, y = p // 8, (p // 4) % 2, p % 4
    zl, c = d // 2, d % 2
    z = zh * 2 + zl
    sig = 1 - 2 * c

    def dev(ax, ay, az, ac):
        return {"doc": (az % 2) * 2 + ac, "param": ax * 8 + (az // 2) * 4 + ay}

    def near(du, dv):
        return dev((x + sig * du + 4) % 4, (y + sig * dv + 4) % 4, z, c)

    sibling = dev(x, y, z, 1 - c)
    own = x * 4 + y

    sends = []
    for t in range(8):
        a = c * 8 + t
        col = ((a // 4) * 8 + (1 - zh) * 4 + a % 4) * 256 + (1 - zl) * 128
        cp = pltpu.make_async_copy(sb.at[:, pl.ds(pl.multiple_of(col, 128), 128)], sts.at[t], ls.at[t])
        cp.start()
        sends.append(cp)
    keeps = []
    for a in range(16):
        col = ((a // 4) * 8 + zh * 4 + a % 4) * 256 + zl * 128
        keeps.append(pltpu.make_async_copy(sb.at[:, pl.ds(pl.multiple_of(col, 128), 128)], stl.at[a], lt.at[a]))

    @pl.when(c == zh)
    def _():
        for cp in keeps:
            cp.start()

    bar = pltpu.get_barrier_semaphore()
    plane = [(i, j) for i in range(4) for j in range(4) if (i, j) != (0, 0)]
    line = [(k, m) for k in range(4) for m in range(2) if (k, m) != (0, 0)]

    def mate(k, m):
        return dev(x, y, (z + k) % 4, (c + m) % 2)

    for i, j in plane:
        pl.semaphore_signal(bar, inc=1, device_id=near(i, j), device_id_type=MESH)
    for k, m in line:
        pl.semaphore_signal(bar, inc=1, device_id=mate(k, m), device_id_type=MESH)

    @pl.when(zl == 0)
    def _():
        gbuf[own, d] = og[:, :128]

    @pl.when(zl == 1)
    def _():
        gbuf[own, d] = og[:, 128:]

    idall[d] = ids[...]
    pl.semaphore_wait(bar, len(plane) + len(line))

    def remote(src, dst, s, r, to):
        return pltpu.make_async_remote_copy(
            src_ref=src, dst_ref=dst, send_sem=s, recv_sem=r, device_id=to, device_id_type=MESH
        )

    pending = []
    count = [0]

    def quarter(piece):
        return (zl if piece == 0 else 1 - zl) * 2 + c

    def slot(u, v):
        return ((x - sig * u + 4) % 4) * 4 + (y - sig * v + 4) % 4

    def pass_on(piece, u, v):
        ref = gbuf.at[slot(u, v), quarter(piece)]
        for du, dv in hops(piece, u, v):
            cp = remote(ref, ref, gs.at[count[0]], gr.at[piece, (u + du) % 4, (v + dv) % 4], near(du, dv))
            count[0] += 1
            cp.start()
            pending.append(cp)
        cp = remote(ref, ref, ss.at[piece, u, v], sr.at[piece, u, v], sibling)
        cp.start()
        pending.append(cp)

    def arrived(piece, u, v):
        ref = gbuf.at[slot(u, v), quarter(piece)]
        remote(ref, ref, ss.at[piece, u, v], gr.at[piece, u, v], sibling).wait_recv()

    ex = remote(
        og.at[:, pl.ds(pl.multiple_of((1 - zl) * 128, 128), 128)], gbuf.at[own, d], gs.at[30], gr.at[1, 0, 0],
        dev(x, y, zh * 2 + 1 - zl, c),
    )
    ex.start()
    pending.append(ex)
    pass_on(0, 0, 0)
    for i, to in enumerate([sibling, dev(x, y, zh * 2 + 1 - zl, c), dev(x, y, zh * 2 + 1 - zl, 1 - c)]):
        cp = remote(ids, idall.at[d], ds_.at[i], dr.at[d], to)
        cp.start()
        pending.append(cp)

    for k in range(1, 4):
        cp = remote(li, xq.at[d], xs_.at[k], xr.at[d], dev(x, y, (z + k) % 4, zh))
        cp.start()
        pending.append(cp)
    near_x = remote(li, xq.at[d], xs_.at[0], xr.at[d], sibling)
    own_x = pltpu.make_async_copy(li, xq.at[d], xl)

    @pl.when(c != zh)
    def _():
        near_x.start()

    @pl.when(c == zh)
    def _():
        own_x.start()

    for t in range(8):
        sends[t].wait()
        sgs[t] = (2 * sts[t] - 1).astype(F32).astype(BF16)
    cp = remote(sgs, sg.at[pl.ds(c * 8, 8)], sgss, sgr.at[c], dev(x, y, (1 - zh) * 2 + 1 - zl, zh))
    cp.start()
    pending.append(cp)

    arrived(1, 0, 0)
    pass_on(1, 0, 0)

    @pl.when(c == zh)
    def _():
        for a in range(16):
            keeps[a].wait()
            sg[a] = (2 * stl[a] - 1).astype(F32).astype(BF16)

    rows, cols = kr[...], kc[...]
    base_v[...] = (((cols >> 11) & 3) * 4 + ((cols >> 8) & 3)) * 256 + (rows & 255)
    lane_v[...] = cols & 127
    rmask = x * 2048 + c * 1024 + y * 256
    cmask = zh * 1024 + zl * 128
    bits = parity((rows & rmask) ^ (cols & cmask))
    sgn_v[...] = (1 - 2 * bits).astype(F32) * (1.0 / 8192)
    to_s = pltpu.make_async_copy(base_v, base_s, km)
    to_s.start()
    hm[...] = sylvester(256)

    def service(step):
        for piece, u, v in WAITS[step]:
            arrived(piece, u, v)
            pass_on(piece, u, v)

    def prepare():
        for q in range(4):
            got = remote(li, xq.at[q], xs_.at[0], xr.at[q], sibling)
            mine = (d == q) & (c == zh)

            @pl.when(mine)
            def _():
                own_x.wait()

            @pl.when(jnp.logical_not(mine))
            def _():
                got.wait_recv()

            @pl.when(d != q)
            def _():
                remote(ids, idall.at[q], ds_.at[0], dr.at[q], sibling).wait_recv()

        big = idall[2][0:1, 0:1]
        for q in range(4):
            idq = idall[q][0:1, :]
            xt = xq[q].astype(F32).T
            xtb[:, q * 512:(q + 1) * 512] = jnp.where(idq == big, xt, 0.0).astype(BF16)
            if q in (0, 3):
                for o in range(3):
                    label = o + (big <= o).astype(I32)
                    col = 0 if q == 0 else 512
                    xto[o * 256:(o + 1) * 256, col:col + 512] = jnp.where(idq == label, xt, 0.0).astype(BF16)

    def pair(one, two):
        for u, v in (one, two):
            for piece in range(2):
                a, b = (-u) % 4, (-v) % 4
                qt = (zl if piece == 0 else 1 - zl) * 2 + 1 - c
                ref = gbuf.at[slot(u, v), qt]
                remote(ref, ref, ss.at[piece, a, b], sr.at[piece, a, b], sibling).wait_recv()
        sa, sb_ = slot(*one), slot(*two)
        w = jnp.concatenate([gbuf[sa].reshape(2048, 128), gbuf[sb_].reshape(2048, 128)], axis=1)
        signs = jnp.concatenate([sg[sa], sg[sb_]], axis=1).astype(F32)
        outer = jnp.concatenate([w[:512], w[1536:]], axis=0)

        for s in range(4):
            if s == 0:
                g = jnp.dot(xtb[...], w, preferred_element_type=F32)
            else:
                g = jnp.dot(xto[(s - 1) * 256:s * 256, :], outer, preferred_element_type=F32)
            hi, lo = halves(g * signs)
            t = jnp.dot(hm[...], hi, preferred_element_type=F32) + jnp.dot(hm[...], lo, preferred_element_type=F32)
            zb[s, sa] = t[:, :128]
            zb[s, sb_] = t[:, 128:]

    for step in range(8):
        service(step)
        if step == 2:
            prepare()

            @pl.when(c != zh)
            def _():
                for h in range(2):
                    remote(sgs, sg.at[pl.ds(h * 8, 8)], sgss, sgr.at[h], sibling).wait_recv()

        for one, two in PAIRS[step]:
            pair(one, two)

    def fly(r, carry):
        for s in range(4):
            v = [zb[s, a, pl.ds(pl.multiple_of(r * 8, 8), 8), :] for a in range(16)]
            h = 1
            while h < 16:
                n = list(v)
                for a in range(16):
                    if a & h == 0:
                        n[a], n[a + h] = v[a] + v[a + h], v[a] - v[a + h]
                v = n
                h *= 2
            for a in range(16):
                z2[pl.ds(a * 256 + r * 8, 8), s, :] = v[a]
        return carry

    lax.fori_loop(0, 32, fly, 0)

    to_s.wait()
    stage = (sa0, sa1, sa2, sa3)
    lanes = lax.broadcasted_iota(I32, (8, 128), 1)
    sub = lax.broadcasted_iota(I32, (128, 128), 0)

    def fetch(t, g):
        for j in range(128):
            t[pl.ds(4 * j, 4), :] = z2[base_s[g, j]]

    def settle(t, g):
        h = (1 - 2 * parity(sub & lane_v[pl.ds(g, 1), :])).astype(F32).astype(BF16)
        hi, lo = halves(t[...])
        r = jnp.dot(
            jnp.concatenate([hi, lo], axis=1), jnp.concatenate([h, h], axis=0), preferred_element_type=F32
        )
        acc = [jnp.zeros((8, 128), F32) for _ in range(4)]
        for q in range(64):
            acc[q % 4] = jnp.where((lanes >> 1) == q, r[8 * q:8 * q + 8, :], acc[q % 4])
        t = (acc[0] + acc[1]) + (acc[2] + acc[3])
        t = jnp.where((lanes[:4] & 1) == 0, t[:4], t[4:])
        for s in range(4):
            ps[s, pl.ds(g, 1), :] = t[s:s + 1, :]

    def pick(i, carry):
        for n in range(4):
            fetch(stage[n], i * 4 + n)
        for n in range(4):
            settle(stage[n], i * 4 + n)
        return carry

    lax.fori_loop(0, 16, pick, 0)

    big = jnp.broadcast_to(idall[2][0:1, 0:1], (64, 128))
    sign = sgn_v[...]
    for e in range(4):
        t = jnp.where(big > e, ps[min(e + 1, 3)], ps[e])
        t = jnp.where(big == e, ps[0], t) * sign
        for h in range(2):
            for i in range(4):
                g0 = (i * 2 + h) * 8
                pd[e * 2 + h, i] = t[g0:g0 + 8, :]
    me8 = d * 2 + zh
    r1[me8] = pd[me8]
    for n, (k, m) in enumerate(line):
        tz, tc = (z + k) % 4, (c + m) % 2
        dest = ((tz % 2) * 2 + tc) * 2 + tz // 2
        cp = remote(pd.at[dest], r1.at[me8], s1.at[n], w1.at[me8], mate(k, m))
        cp.start()
        pending.append(cp)
    for k, m in line:
        tz, tc = (z + k) % 4, (c + m) % 2
        src = ((tz % 2) * 2 + tc) * 2 + tz // 2
        remote(pd.at[src], r1.at[src], s1.at[0], w1.at[src], sibling).wait_recv()
    for i in range(4):
        t = r1[0, i]
        for n in range(1, 8):
            t = t + r1[n, i]
        for j in range(4):
            q2[i * 4 + j, 0:2, :] = t[2 * j:2 * j + 2, :]
            q2[i * 4 + j, 2:8, :] = jnp.zeros((6, 128), F32)
    r2[own] = q2[own]
    for n, (i, j) in enumerate(plane):
        dest = ((x + sig * i + 4) % 4) * 4 + (y + sig * j + 4) % 4
        cp = remote(q2.at[dest], r2.at[own], s2.at[n], w2.at[own], near(i, j))
        cp.start()
        pending.append(cp)
    for i, j in plane:
        src = ((x + sig * i + 4) % 4) * 4 + (y + sig * j + 4) % 4
        remote(q2.at[src], r2.at[src], s2.at[0], w2.at[src], sibling).wait_recv()
    t = r2[0]
    for n in range(1, 16):
        t = t + r2[n]
    out[...] = t

    @pl.when(c != zh)
    def _():
        near_x.wait_send()

    for cp in pending:
        cp.wait_send()


def on_device(layer_input, output_grad, doc_ids, sign_bits, kept_rows, kept_cols):
    vm = pl.BlockSpec(memory_space=pltpu.VMEM)
    dma = pltpu.SemaphoreType.DMA
    scratch = [
        pltpu.VMEM((16, 4, 512, 128), BF16),
        pltpu.VMEM((4, 16, 256, 128), F32),
        pltpu.VMEM((4096, 4, 128), F32),
        pltpu.VMEM((4, 512, 256), BF16),
        pltpu.VMEM((256, 2048), BF16),
        pltpu.VMEM((768, 1024), BF16),
        pltpu.VMEM((16, 256, 128), BF16),
        pltpu.VMEM((16, 256, 128), I32),
        pltpu.VMEM((8, 256, 128), I32),
        pltpu.VMEM((8, 256, 128), BF16),
        pltpu.VMEM((4, 8, 512), I32),
        pltpu.VMEM((256, 256), BF16),
        pltpu.VMEM((64, 128), I32),
        pltpu.VMEM((64, 128), I32),
        pltpu.VMEM((64, 128), F32),
        pltpu.SMEM((64, 128), I32),
        pltpu.VMEM((512, 128), F32),
        pltpu.VMEM((512, 128), F32),
        pltpu.VMEM((512, 128), F32),
        pltpu.VMEM((512, 128), F32),
        pltpu.VMEM((4, 64, 128), F32),
        pltpu.VMEM((8, 4, 8, 128), F32),
        pltpu.VMEM((8, 4, 8, 128), F32),
        pltpu.VMEM((16, 8, 128), F32),
        pltpu.VMEM((16, 8, 128), F32),
        dma((31,)), dma((2, 4, 4)), dma((2, 4, 4)), dma((2, 4, 4)),
        dma((4,)), dma((4,)), dma(()), dma((3,)), dma((4,)),
        dma((8,)), dma((16,)), dma(()), dma((2,)), dma(()),
        dma((7,)), dma((8,)), dma((15,)), dma((16,)),
    ]
    got = pl.pallas_call(
        kernel,
        out_shape=jax.ShapeDtypeStruct((8, 128), F32),
        in_specs=[vm, vm, vm, pl.BlockSpec(memory_space=pl.ANY), vm, vm],
        out_specs=vm,
        scratch_shapes=scratch,
        compiler_params=pltpu.CompilerParams(
            collective_id=0, has_side_effects=True, vmem_limit_bytes=60 << 20
        ),
        name="sketch",
    )(
        layer_input, output_grad, jnp.broadcast_to(doc_ids[None, :], (8, 512)), sign_bits,
        kept_rows.reshape(64, 128), kept_cols.reshape(64, 128),
    )
    return got[:2].reshape(1, 256)


def solution(mesh):
    placed = (P("doc", "param"), P("doc", "param"), P("doc"), P("param", None), P(), P())
    return jax.shard_map(
        on_device, mesh=mesh, in_specs=placed, out_specs=P("doc", "param"), check_vma=False
    )
```

```python
import functools

import jax
import jax.numpy as jnp
from jax import lax
from jax.experimental import pallas as pl
from jax.experimental.pallas import tpu as pltpu
from jax.sharding import PartitionSpec as P

MESH = pl.DeviceIdType.MESH
F32, BF16, I32 = jnp.float32, jnp.bfloat16, jnp.int32

WAITS = [
    [(0, 1, 0), (0, 3, 0), (1, 0, 1), (1, 0, 3)],
    [(0, 2, 0), (1, 0, 2), (0, 0, 1), (1, 1, 0)],
    [(0, 1, 1), (1, 1, 1), (0, 3, 1), (1, 1, 3)],
    [(0, 2, 1), (1, 1, 2), (0, 0, 3), (1, 3, 0)],
    [(0, 1, 3), (1, 3, 1), (0, 3, 3), (1, 3, 3)],
    [(0, 2, 3), (1, 3, 2), (0, 0, 2), (1, 2, 0)],
    [(0, 1, 2), (1, 2, 1), (0, 3, 2), (1, 2, 3)],
    [(0, 2, 2), (1, 2, 2)],
]
PAIRS = [
    ((1, 0), (3, 0)), ((0, 1), (0, 3)), ((1, 1), (3, 3)), ((1, 3), (3, 1)),
    ((0, 0), (2, 0)), ((2, 1), (2, 3)), ((1, 2), (3, 2)), ((0, 2), (2, 2)),
]
READY = {3: (0, 1), 4: (2, 3), 5: (4,), 6: (5, 6), 7: (7,)}


def hops(piece, u, v):
    a, b = (u, v) if piece == 0 else (v, u)
    if (a, b) == (0, 0):
        out = [(1, 0), (3, 0), (0, 1), (0, 3)]
    elif b == 0:
        out = ([(1, 0)] if a == 1 else []) + [(0, 1), (0, 3)]
    elif b == 1:
        out = [(0, 1)]
    else:
        out = []
    return out if piece == 0 else [(d, c) for c, d in out]


def parity(t):
    for s in (8, 4):
        t = t ^ (t >> s)
    return (jnp.int32(0x6996) >> (t & 15)) & 1


def sylvester(n):
    i = lax.broadcasted_iota(I32, (n, n), 0)
    j = lax.broadcasted_iota(I32, (n, n), 1)
    return (1 - 2 * parity(i & j)).astype(F32).astype(BF16)


def halves(t):
    hi = t.astype(BF16)
    lo = (t - hi.astype(F32)).astype(BF16)
    return hi, lo


def kernel(
    li, og, ids, sb, kr, kc, out,
    gbuf, zb, z2, xq, xtb, xto, sg, stl, sts, sgs, idall, hm, mcol, lane_v, base_v, sgn_v, base_a, base_b,
    sa0, sa1, sa2, sa3, ps, pd, r1, q2, r2,
    gs, gr, ss, sr, xs_, xr, xl, ds_, dr, ls, lt, sgss, sgr, km, s1, w1, s2, w2,
):
    d = lax.axis_index("doc")
    p = lax.axis_index("param")
    x, zh, y = p // 8, (p // 4) % 2, p % 4
    zl, c = d // 2, d % 2
    z = zh * 2 + zl
    sig = 1 - 2 * c

    def dev(ax, ay, az, ac):
        return {"doc": (az % 2) * 2 + ac, "param": ax * 8 + (az // 2) * 4 + ay}

    def near(du, dv):
        return dev((x + sig * du + 4) % 4, (y + sig * dv + 4) % 4, z, c)

    sibling = dev(x, y, z, 1 - c)
    own = x * 4 + y

    bar = pltpu.get_barrier_semaphore()
    plane = [(i, j) for i in range(4) for j in range(4) if (i, j) != (0, 0)]
    line = [(k, m) for k in range(4) for m in range(2) if (k, m) != (0, 0)]

    def mate(k, m):
        return dev(x, y, (z + k) % 4, (c + m) % 2)

    for i, j in plane:
        pl.semaphore_signal(bar, inc=1, device_id=near(i, j), device_id_type=MESH)
    for k, m in line:
        pl.semaphore_signal(bar, inc=1, device_id=mate(k, m), device_id_type=MESH)

    def column(a, h, l):
        return pl.multiple_of(((a // 4) * 8 + h * 4 + a % 4) * 256 + l * 128, 128)

    def far_slot(u, v):
        f = 1 - 2 * zh
        return ((x - f * u + 4) % 4) * 4 + (y - f * v + 4) % 4

    sends = []
    for t in range(8):
        a = jnp.where(c == 0, far_slot(*PAIRS[t][0]), far_slot(*PAIRS[t][1]))
        cp = pltpu.make_async_copy(sb.at[:, pl.ds(column(a, 1 - zh, 1 - zl), 128)], sts.at[t], ls.at[t])
        cp.start()
        sends.append((a, cp))
    keeps = []
    for a in range(16):
        keeps.append(pltpu.make_async_copy(sb.at[:, pl.ds(column(a, zh, zl), 128)], stl.at[a], lt.at[a]))

    @pl.when(c == zh)
    def _():
        for cp in keeps:
            cp.start()

    @pl.when(zl == 0)
    def _():
        gbuf[own, d] = og[:, :128]

    @pl.when(zl == 1)
    def _():
        gbuf[own, d] = og[:, 128:]

    idall[d] = ids[...]
    pl.semaphore_wait(bar, len(plane) + len(line))

    def remote(src, dst, s, r, to):
        return pltpu.make_async_remote_copy(
            src_ref=src, dst_ref=dst, send_sem=s, recv_sem=r, device_id=to, device_id_type=MESH
        )

    pending = []
    count = [0]

    def quarter(piece):
        return (zl if piece == 0 else 1 - zl) * 2 + c

    def slot(u, v):
        return ((x - sig * u + 4) % 4) * 4 + (y - sig * v + 4) % 4

    def pass_on(piece, u, v):
        ref = gbuf.at[slot(u, v), quarter(piece)]
        for du, dv in hops(piece, u, v):
            cp = remote(ref, ref, gs.at[count[0]], gr.at[piece, (u + du) % 4, (v + dv) % 4], near(du, dv))
            count[0] += 1
            cp.start()
            pending.append(cp)
        cp = remote(ref, ref, ss.at[piece, u, v], sr.at[piece, u, v], sibling)
        cp.start()
        pending.append(cp)

    def arrived(piece, u, v):
        ref = gbuf.at[slot(u, v), quarter(piece)]
        remote(ref, ref, ss.at[piece, u, v], gr.at[piece, u, v], sibling).wait_recv()

    ex = remote(
        og.at[:, pl.ds(pl.multiple_of((1 - zl) * 128, 128), 128)], gbuf.at[own, d], gs.at[30], gr.at[1, 0, 0],
        dev(x, y, zh * 2 + 1 - zl, c),
    )
    ex.start()
    pending.append(ex)
    pass_on(0, 0, 0)
    for i, to in enumerate([sibling, dev(x, y, zh * 2 + 1 - zl, c), dev(x, y, zh * 2 + 1 - zl, 1 - c)]):
        cp = remote(ids, idall.at[d], ds_.at[i], dr.at[d], to)
        cp.start()
        pending.append(cp)

    beside, across = zh * 2 + 1 - zl, (1 - zh) * 2 + 1 - zl
    x_over = remote(li, xq.at[d], xs_.at[2], xr.at[d], dev(x, y, across, zh))
    x_over.start()
    x_side = remote(li, xq.at[d], xs_.at[1], xr.at[d], dev(x, y, beside, zh))
    x_side.start()
    near_x = remote(li, xq.at[d], xs_.at[0], xr.at[d], sibling)
    own_x = pltpu.make_async_copy(li, xq.at[d], xl)

    @pl.when(c != zh)
    def _():
        near_x.start()

    @pl.when(c == zh)
    def _():
        own_x.start()

    relays = []
    for k in range(2):
        ref = xq.at[(1 - zl) * 2 + k]
        relays.append(remote(ref, ref, xs_.at[3 + k], xr.at[(1 - zl) * 2 + k], dev(x, y, beside, c)))

    for t in range(8):
        sends[t][1].wait()
        sgs[t] = (2 * sts[t] - 1).astype(F32).astype(BF16)

    def send_signs():
        for k in range(2):
            @pl.when(c != zh)
            def _():
                relays[k].wait_recv()
                relays[k].start()
        x_over.wait_send()
        for t in range(8):
            cp = remote(sgs.at[t], sg.at[sends[t][0]], sgss.at[t], sgr.at[t, c], dev(x, y, across, zh))
            cp.start()
            pending.append(cp)

    arrived(1, 0, 0)
    pass_on(1, 0, 0)

    @pl.when(c == zh)
    def _():
        for a in range(16):
            keeps[a].wait()
            sg[a] = (2 * stl[a] - 1).astype(F32).astype(BF16)

    rows, cols = kr[...], kc[...]
    base_v[...] = ((((cols >> 11) & 3) * 4 + ((cols >> 8) & 3)) * 256 + (rows & 255)) * 4
    lane_v[...] = cols & 127
    rmask = x * 2048 + c * 1024 + y * 256
    cmask = zh * 1024 + zl * 128
    bits = parity((rows & rmask) ^ (cols & cmask))
    sgn_v[...] = (1 - 2 * bits).astype(F32) * (1.0 / 8192)
    def index_a(i):
        return pltpu.make_async_copy(base_v.at[i], base_a, km.at[0])

    def index_b(i):
        return pltpu.make_async_copy(base_v.at[i], base_b, km.at[1])

    index_a(0).start()
    index_b(1).start()
    hm[...] = sylvester(256)

    def service(step):
        for piece, u, v in WAITS[step]:
            arrived(piece, u, v)
            pass_on(piece, u, v)

    def prepare():
        for q in range(4):
            got = remote(li, xq.at[q], xs_.at[0], xr.at[q], sibling)
            mine = (d == q) & (c == zh)
            seen = (c != zh) & ((q // 2) != zl)

            @pl.when(mine)
            def _():
                own_x.wait()

            @pl.when(jnp.logical_not(mine | seen))
            def _():
                got.wait_recv()

            @pl.when(d != q)
            def _():
                remote(ids, idall.at[q], ds_.at[0], dr.at[q], sibling).wait_recv()

        def labels(q):
            return jnp.concatenate([idall[q, i:i + 1, :] for i in range(4)], axis=1)

        big = idall[2, 0:1, 0:1]
        id0, id3 = labels(0), labels(3)
        short = id0 != big
        x0, x3 = xq[0].astype(F32).T, xq[3].astype(F32).T
        xtb[:, 0:512] = xq[1].astype(F32).T.astype(BF16)
        xtb[:, 512:1024] = xq[2].astype(F32).T.astype(BF16)
        xtb[:, 1024:1536] = jnp.where(short, x3, x0).astype(BF16)
        rest, id_rest = jnp.where(short, x0, x3), jnp.where(short, id0, id3)
        for o in range(3):
            label = o + (big <= o).astype(I32)
            xto[o * 256:(o + 1) * 256, :] = jnp.where(id_rest == label, rest, 0.0).astype(BF16)
        side = jnp.broadcast_to(short.astype(F32), (128, 512)).T.astype(BF16)
        mcol[...] = jnp.concatenate([side, side], axis=1)

    def pair(n):
        one, two = PAIRS[n]
        for u, v in (one, two):
            for piece in range(2):
                a, b = (-u) % 4, (-v) % 4
                qt = (zl if piece == 0 else 1 - zl) * 2 + 1 - c
                ref = gbuf.at[slot(u, v), qt]
                remote(ref, ref, ss.at[piece, a, b], sr.at[piece, a, b], sibling).wait_recv()
        sa, sb_ = slot(*one), slot(*two)

        @pl.when(c != zh)
        def _():
            for h, a in enumerate((sa, sb_)):
                remote(sgs.at[0], sg.at[a], sgss.at[0], sgr.at[n, h], sibling).wait_recv()

        w = [jnp.concatenate([gbuf[sa, q], gbuf[sb_, q]], axis=1) for q in range(4)]
        signs = jnp.concatenate([sg[sa], sg[sb_]], axis=1).astype(F32)
        short = mcol[...] != 0
        long_w = jnp.concatenate([w[1], w[2], jnp.where(short, w[3], w[0])], axis=0)
        g0 = jnp.dot(xtb[...], long_w, preferred_element_type=F32)
        g1 = jnp.dot(xto[...], jnp.where(short, w[0], w[3]), preferred_element_type=F32)
        for s in range(4):
            g = g0 if s == 0 else g1[(s - 1) * 256:s * 256]
            hi, lo = halves(g * signs)
            t = jnp.dot(hm[...], hi, preferred_element_type=F32) + jnp.dot(hm[...], lo, preferred_element_type=F32)
            zb[s, sa] = t[:, :128]
            zb[s, sb_] = t[:, 128:]

    for step in range(8):
        service(step)
        if step == 1:
            send_signs()
        if step == 3:
            prepare()
        for n in READY.get(step, ()):
            pair(n)

    def fly(r, carry):
        for s in range(4):
            v = [zb[s, a, pl.ds(pl.multiple_of(r * 8, 8), 8), :] for a in range(16)]
            h = 1
            while h < 16:
                n = list(v)
                for a in range(16):
                    if a & h == 0:
                        n[a], n[a + h] = v[a] + v[a + h], v[a] - v[a + h]
                v = n
                h *= 2
            for a in range(16):
                z2[pl.ds(a * 1024 + r * 32 + s, 8, stride=4), :] = v[a]
        return carry

    lax.fori_loop(0, 32, fly, 0)

    stage = (sa0, sa1, sa2, sa3)
    lanes = lax.broadcasted_iota(I32, (8, 128), 1)
    sub = lax.broadcasted_iota(I32, (128, 128), 0)

    def fetch(t, base, n):
        for j in range(128):
            t[pl.ds(4 * j, 4), :] = z2[pl.ds(base[n, j], 4), :]

    def settle(t, i, n):
        h = jnp.where(parity(sub & lane_v[i, n:n + 1, :]) == 1, -1.0, 1.0).astype(BF16)
        hi, lo = halves(t[...])
        r = jnp.dot(
            jnp.concatenate([hi, lo], axis=1), jnp.concatenate([h, h], axis=0), preferred_element_type=F32
        )
        acc = [jnp.zeros((8, 128), F32) for _ in range(4)]
        for q in range(64):
            acc[q % 4] = jnp.where((lanes >> 1) == q, r[8 * q:8 * q + 8, :], acc[q % 4])
        t = (acc[0] + acc[1]) + (acc[2] + acc[3])
        t = jnp.where((lanes[:4] & 1) == 0, t[:4], t[4:])
        for s in range(4):
            ps[s, i, n:n + 1, :] = t[s:s + 1, :]

    def pick(i, carry):
        for k, (index, base) in enumerate(((index_a, base_a), (index_b, base_b))):
            m = 2 * i + k
            index(m).wait()
            for n in range(4):
                fetch(stage[n], base, n)
            index(jnp.minimum(m + 2, 15)).start()
            for n in range(4):
                settle(stage[n], m, n)
        return carry

    lax.fori_loop(0, 8, pick, 0)
    index_a(0).wait()
    index_b(0).wait()

    big = jnp.broadcast_to(idall[2, 0:1, 0:1], (16, 4, 128))
    sign = sgn_v[...]
    for e in range(4):
        t = jnp.where(big > e, ps[min(e + 1, 3)], ps[e])
        t = jnp.where(big == e, ps[0], t) * sign
        for h in range(2):
            for i in range(4):
                pd[e * 2 + h, i, 0:4] = t[i * 4 + h * 2]
                pd[e * 2 + h, i, 4:8] = t[i * 4 + h * 2 + 1]
    me8 = d * 2 + zh
    r1[me8] = pd[me8]
    for n, (k, m) in enumerate(line):
        tz, tc = (z + k) % 4, (c + m) % 2
        dest = ((tz % 2) * 2 + tc) * 2 + tz // 2
        cp = remote(pd.at[dest], r1.at[me8], s1.at[n], w1.at[me8], mate(k, m))
        cp.start()
        pending.append(cp)
    for k, m in line:
        tz, tc = (z + k) % 4, (c + m) % 2
        src = ((tz % 2) * 2 + tc) * 2 + tz // 2
        remote(pd.at[src], r1.at[src], s1.at[0], w1.at[src], sibling).wait_recv()
    for i in range(4):
        t = r1[0, i]
        for n in range(1, 8):
            t = t + r1[n, i]
        for j in range(4):
            q2[i * 4 + j, 0:2, :] = t[2 * j:2 * j + 2, :]
            q2[i * 4 + j, 2:8, :] = jnp.zeros((6, 128), F32)
    r2[own] = q2[own]
    for n, (i, j) in enumerate(plane):
        dest = ((x + sig * i + 4) % 4) * 4 + (y + sig * j + 4) % 4
        cp = remote(q2.at[dest], r2.at[own], s2.at[n], w2.at[own], near(i, j))
        cp.start()
        pending.append(cp)
    for i, j in plane:
        src = ((x + sig * i + 4) % 4) * 4 + (y + sig * j + 4) % 4
        remote(q2.at[src], r2.at[src], s2.at[0], w2.at[src], sibling).wait_recv()
    t = r2[0]
    for n in range(1, 16):
        t = t + r2[n]
    out[...] = t

    @pl.when(c != zh)
    def _():
        near_x.wait_send()
        for cp in relays:
            cp.wait_send()

    x_side.wait_send()
    for cp in pending:
        cp.wait_send()


def on_device(layer_input, output_grad, doc_ids, sign_bits, kept_rows, kept_cols):
    vm = pl.BlockSpec(memory_space=pltpu.VMEM)
    dma = pltpu.SemaphoreType.DMA
    scratch = [
        pltpu.VMEM((16, 4, 512, 128), BF16),
        pltpu.VMEM((4, 16, 256, 128), F32),
        pltpu.VMEM((16384, 128), F32),
        pltpu.VMEM((4, 512, 256), BF16),
        pltpu.VMEM((256, 1536), BF16),
        pltpu.VMEM((768, 512), BF16),
        pltpu.VMEM((16, 256, 128), BF16),
        pltpu.VMEM((16, 256, 128), I32),
        pltpu.VMEM((8, 256, 128), I32),
        pltpu.VMEM((8, 256, 128), BF16),
        pltpu.VMEM((4, 4, 128), I32),
        pltpu.VMEM((256, 256), BF16),
        pltpu.VMEM((512, 256), BF16),
        pltpu.VMEM((16, 4, 128), I32),
        pltpu.VMEM((16, 4, 128), I32),
        pltpu.VMEM((16, 4, 128), F32),
        pltpu.SMEM((4, 128), I32),
        pltpu.SMEM((4, 128), I32),
        pltpu.VMEM((512, 128), F32),
        pltpu.VMEM((512, 128), F32),
        pltpu.VMEM((512, 128), F32),
        pltpu.VMEM((512, 128), F32),
        pltpu.VMEM((4, 16, 4, 128), F32),
        pltpu.VMEM((8, 4, 8, 128), F32),
        pltpu.VMEM((8, 4, 8, 128), F32),
        pltpu.VMEM((16, 8, 128), F32),
        pltpu.VMEM((16, 8, 128), F32),
        dma((31,)), dma((2, 4, 4)), dma((2, 4, 4)), dma((2, 4, 4)),
        dma((5,)), dma((4,)), dma(()), dma((3,)), dma((4,)),
        dma((8,)), dma((16,)), dma((8,)), dma((8, 2)), dma((2,)),
        dma((7,)), dma((8,)), dma((15,)), dma((16,)),
    ]
    got = pl.pallas_call(
        kernel,
        out_shape=jax.ShapeDtypeStruct((8, 128), F32),
        in_specs=[vm, vm, vm, pl.BlockSpec(memory_space=pl.ANY), vm, vm],
        out_specs=vm,
        scratch_shapes=scratch,
        compiler_params=pltpu.CompilerParams(
            collective_id=0, has_side_effects=True, vmem_limit_bytes=60 << 20
        ),
        name="sketch",
    )(
        layer_input, output_grad, doc_ids.reshape(4, 128), sign_bits,
        kept_rows.reshape(16, 4, 128), kept_cols.reshape(16, 4, 128),
    )
    return got[:2].reshape(1, 256)


def solution(mesh):
    placed = (P("doc", "param"), P("doc", "param"), P("doc"), P("param", None), P(), P())
    return jax.shard_map(
        on_device, mesh=mesh, in_specs=placed, out_specs=P("doc", "param"), check_vma=False
    )
```

```python
import functools

import jax
import jax.numpy as jnp
from jax import lax
from jax.experimental import pallas as pl
from jax.experimental.pallas import tpu as pltpu
from jax.sharding import PartitionSpec as P

MESH = pl.DeviceIdType.MESH
F32, BF16, I32 = jnp.float32, jnp.bfloat16, jnp.int32

PAIRS = [
    ((1, 0), (3, 0)), ((0, 1), (0, 3)), ((1, 1), (3, 3)), ((1, 3), (3, 1)),
    ((0, 0), (2, 0)), ((2, 1), (2, 3)), ((1, 2), (3, 2)), ((0, 2), (2, 2)),
]
OPS = [
    (1, 0, 0), (0, 1, 0), (0, 3, 0), "relay", (1, 0, 1), (1, 0, 3), "signs", (0, 2, 0), (1, 0, 2), (0, 0, 1),
    (1, 1, 0), (0, 1, 1), (1, 1, 1), (0, 3, 1), (1, 1, 3), (0, 0, 3), (1, 3, 0), "inputs", 0, 1, (0, 2, 1), (1, 1, 2),
    (0, 1, 3), (1, 3, 1), (0, 3, 3), (1, 3, 3), 2, 3, (0, 2, 3), (1, 3, 2), (0, 0, 2), (1, 2, 0), 4, (0, 1, 2),
    (1, 2, 1), (0, 3, 2), (1, 2, 3), 5, 6, (0, 2, 2), (1, 2, 2), 7,
]


def hops(piece, u, v):
    a, b = (u, v) if piece == 0 else (v, u)
    if (a, b) == (0, 0):
        out = [(1, 0), (3, 0), (0, 1), (0, 3)]
    elif b == 0:
        out = ([(1, 0)] if a == 1 else []) + [(0, 1), (0, 3)]
    elif b == 1:
        out = [(0, 1)]
    else:
        out = []
    return out if piece == 0 else [(d, c) for c, d in out]


def parity(t):
    for s in (8, 4):
        t = t ^ (t >> s)
    return (jnp.int32(0x6996) >> (t & 15)) & 1


def sylvester(n):
    i = lax.broadcasted_iota(I32, (n, n), 0)
    j = lax.broadcasted_iota(I32, (n, n), 1)
    return (1 - 2 * parity(i & j)).astype(F32).astype(BF16)


def halves(t):
    hi = t.astype(BF16)
    lo = (t - hi.astype(F32)).astype(BF16)
    return hi, lo


def kernel(
    li, og, ids, sb, kr, kc, out,
    kr_v, kc_v, gbuf, zb, z2, xq, xtb, xto, sg, stl, sts, sgs, idall, hm, mcol, lane_v, base_v, sgn_v, base_a, base_b,
    sa0, sa1, sa2, sa3, sa4, sa5, sa6, sa7, ps, pd, r1, q2, r2,
    lo_, gs, gr, ss, sr, xs_, xr, xl, ds_, dr, ls, lt, sgss, sgr, km, s1, w1, s2, w2,
):
    d = lax.axis_index("doc")
    p = lax.axis_index("param")
    x, zh, y = p // 8, (p // 4) % 2, p % 4
    zl, c = d // 2, d % 2
    z = zh * 2 + zl
    sig = 1 - 2 * c

    def dev(ax, ay, az, ac):
        return {"doc": (az % 2) * 2 + ac, "param": ax * 8 + (az // 2) * 4 + ay}

    def near(du, dv):
        return dev((x + sig * du + 4) % 4, (y + sig * dv + 4) % 4, z, c)

    sibling = dev(x, y, z, 1 - c)
    own = x * 4 + y

    bar = pltpu.get_barrier_semaphore()
    plane = [(i, j) for i in range(4) for j in range(4) if (i, j) != (0, 0)]
    ring = [(1, 0), (3, 0), (0, 1), (0, 3)]
    line = [(k, m) for k in range(4) for m in range(2) if (k, m) != (0, 0)]

    def mate(k, m):
        return dev(x, y, (z + k) % 4, (c + m) % 2)

    for i, j in ring:
        pl.semaphore_signal(bar, inc=1, device_id=near(i, j), device_id_type=MESH)
    for k, m in line:
        pl.semaphore_signal(bar, inc=1, device_id=mate(k, m), device_id_type=MESH)

    def half(l):
        return og.at[:, pl.ds(pl.multiple_of(l * 128, 128), 128)]

    own_g = pltpu.make_async_copy(half(zl), gbuf.at[own, d], lo_.at[0])
    own_i = pltpu.make_async_copy(ids, idall.at[d], lo_.at[1])
    own_r = pltpu.make_async_copy(kr, kr_v, lo_.at[2])
    own_c = pltpu.make_async_copy(kc, kc_v, lo_.at[3])
    for cp in (own_g, own_i, own_r, own_c):
        cp.start()

    def column(a, h, l):
        return pl.multiple_of(((a // 4) * 8 + h * 4 + a % 4) * 256 + l * 128, 128)

    def far_slot(u, v):
        f = 1 - 2 * zh
        return ((x - f * u + 4) % 4) * 4 + (y - f * v + 4) % 4

    sends = []
    for t in range(8):
        a = jnp.where(c == 0, far_slot(*PAIRS[t][0]), far_slot(*PAIRS[t][1]))
        cp = pltpu.make_async_copy(sb.at[:, pl.ds(column(a, 1 - zh, 1 - zl), 128)], sts.at[t], ls.at[t])
        cp.start()
        sends.append((a, cp))
    keeps = []
    for a in range(16):
        keeps.append(pltpu.make_async_copy(sb.at[:, pl.ds(column(a, zh, zl), 128)], stl.at[a], lt.at[a]))

    @pl.when(c == zh)
    def _():
        for cp in keeps:
            cp.start()

    pl.semaphore_wait(bar, len(ring) + len(line))

    def remote(src, dst, s, r, to):
        return pltpu.make_async_remote_copy(
            src_ref=src, dst_ref=dst, send_sem=s, recv_sem=r, device_id=to, device_id_type=MESH
        )

    pending = []
    count = [0]

    def quarter(piece):
        return (zl if piece == 0 else 1 - zl) * 2 + c

    def slot(u, v):
        return ((x - sig * u + 4) % 4) * 4 + (y - sig * v + 4) % 4

    def pass_on(piece, u, v):
        ref = gbuf.at[slot(u, v), quarter(piece)]
        src = half(zl) if (piece, u, v) == (0, 0, 0) else ref
        for du, dv in hops(piece, u, v):
            cp = remote(src, ref, gs.at[count[0]], gr.at[piece, (u + du) % 4, (v + dv) % 4], near(du, dv))
            count[0] += 1
            cp.start()
            pending.append(cp)
        cp = remote(src, ref, ss.at[piece, u, v], sr.at[piece, u, v], sibling)
        cp.start()
        pending.append(cp)

    def arrived(piece, u, v):
        ref = gbuf.at[slot(u, v), quarter(piece)]
        remote(ref, ref, ss.at[piece, u, v], gr.at[piece, u, v], sibling).wait_recv()

    ex = remote(
        half(1 - zl), gbuf.at[own, d], gs.at[30], gr.at[1, 0, 0],
        dev(x, y, zh * 2 + 1 - zl, c),
    )
    ex.start()
    pending.append(ex)
    pass_on(0, 0, 0)
    for i, to in enumerate([sibling, dev(x, y, zh * 2 + 1 - zl, c), dev(x, y, zh * 2 + 1 - zl, 1 - c)]):
        cp = remote(ids, idall.at[d], ds_.at[i], dr.at[d], to)
        cp.start()
        pending.append(cp)

    beside, across = zh * 2 + 1 - zl, (1 - zh) * 2 + 1 - zl
    x_over = remote(li, xq.at[d], xs_.at[2], xr.at[d], dev(x, y, across, zh))
    x_over.start()
    x_side = remote(li, xq.at[d], xs_.at[1], xr.at[d], dev(x, y, beside, zh))
    x_side.start()
    near_x = remote(li, xq.at[d], xs_.at[0], xr.at[d], sibling)
    own_x = pltpu.make_async_copy(li, xq.at[d], xl)

    @pl.when(c != zh)
    def _():
        near_x.start()

    @pl.when(c == zh)
    def _():
        own_x.start()

    relays = []
    for k in range(2):
        ref = xq.at[(1 - zl) * 2 + k]
        relays.append(remote(ref, ref, xs_.at[3 + k], xr.at[(1 - zl) * 2 + k], dev(x, y, beside, c)))

    for t in range(8):
        sends[t][1].wait()
        sgs[t] = (2 * sts[t] - 1).astype(F32).astype(BF16)

    def relay():
        for k in range(2):
            @pl.when(c != zh)
            def _():
                relays[k].wait_recv()
                relays[k].start()

    def send_signs():
        for t in range(8):
            cp = remote(sgs.at[t], sg.at[sends[t][0]], sgss.at[t], sgr.at[t, c], dev(x, y, across, zh))
            cp.start()
            pending.append(cp)


    @pl.when(c == zh)
    def _():
        for a in range(16):
            keeps[a].wait()
            sg[a] = (2 * stl[a] - 1).astype(F32).astype(BF16)

    own_r.wait()
    own_c.wait()
    rows, cols = kr_v[...], kc_v[...]
    base_v[...] = ((((cols >> 11) & 3) * 4 + ((cols >> 8) & 3)) * 256 + (rows & 255)) * 4
    lane_v[...] = cols & 127
    rmask = x * 2048 + c * 1024 + y * 256
    cmask = zh * 1024 + zl * 128
    bits = parity((rows & rmask) ^ (cols & cmask))
    sgn_v[...] = (1 - 2 * bits).astype(F32) * (1.0 / 8192)
    def index_a(i):
        return pltpu.make_async_copy(base_v.at[i], base_a, km.at[0])

    def index_b(i):
        return pltpu.make_async_copy(base_v.at[i], base_b, km.at[1])

    index_a(0).start()
    index_b(1).start()
    hm[...] = sylvester(256)

    def prepare():
        for q in range(4):
            got = remote(li, xq.at[q], xs_.at[0], xr.at[q], sibling)
            mine = (d == q) & (c == zh)
            seen = (c != zh) & ((q // 2) != zl)

            @pl.when(mine)
            def _():
                own_x.wait()

            @pl.when(jnp.logical_not(mine | seen))
            def _():
                got.wait_recv()

            @pl.when(d == q)
            def _():
                own_i.wait()

            @pl.when(d != q)
            def _():
                remote(ids, idall.at[q], ds_.at[0], dr.at[q], sibling).wait_recv()

        def labels(q):
            return jnp.concatenate([idall[q, i:i + 1, :] for i in range(4)], axis=1)

        big = idall[2, 0:1, 0:1]
        id0, id3 = labels(0), labels(3)
        short = id0 != big
        x0, x3 = xq[0].astype(F32).T, xq[3].astype(F32).T
        xtb[:, 0:512] = xq[1].astype(F32).T.astype(BF16)
        xtb[:, 512:1024] = xq[2].astype(F32).T.astype(BF16)
        xtb[:, 1024:1536] = jnp.where(short, x3, x0).astype(BF16)
        rest, id_rest = jnp.where(short, x0, x3), jnp.where(short, id0, id3)
        for o in range(3):
            label = o + (big <= o).astype(I32)
            xto[o * 256:(o + 1) * 256, :] = jnp.where(id_rest == label, rest, 0.0).astype(BF16)
        side = jnp.broadcast_to(short.astype(F32), (128, 512)).T.astype(BF16)
        mcol[...] = jnp.concatenate([side, side], axis=1)

    def pair(n):
        one, two = PAIRS[n]
        for u, v in (one, two):
            for piece in range(2):
                a, b = (-u) % 4, (-v) % 4
                qt = (zl if piece == 0 else 1 - zl) * 2 + 1 - c
                ref = gbuf.at[slot(u, v), qt]
                remote(ref, ref, ss.at[piece, a, b], sr.at[piece, a, b], sibling).wait_recv()
        sa, sb_ = slot(*one), slot(*two)

        @pl.when(c != zh)
        def _():
            for h, a in enumerate((sa, sb_)):
                remote(sgs.at[0], sg.at[a], sgss.at[0], sgr.at[n, h], sibling).wait_recv()

        w = [jnp.concatenate([gbuf[sa, q], gbuf[sb_, q]], axis=1) for q in range(4)]
        signs = jnp.concatenate([sg[sa], sg[sb_]], axis=1).astype(F32)
        short = mcol[...] != 0
        long_w = jnp.concatenate([w[1], w[2], jnp.where(short, w[3], w[0])], axis=0)
        g0 = jnp.dot(xtb[...], long_w, preferred_element_type=F32)
        g1 = jnp.dot(xto[...], jnp.where(short, w[0], w[3]), preferred_element_type=F32)
        for s in range(4):
            g = g0 if s == 0 else g1[(s - 1) * 256:s * 256]
            hi, lo = halves(g * signs)
            t = jnp.dot(hm[...], hi, preferred_element_type=F32) + jnp.dot(hm[...], lo, preferred_element_type=F32)
            zb[s, sa] = t[:, :128]
            zb[s, sb_] = t[:, 128:]

    own_g.wait()
    for op in OPS:
        if op == "signs":
            send_signs()
        elif op == "relay":
            relay()
        elif op == "inputs":
            prepare()
        elif isinstance(op, int):
            pair(op)
        else:
            arrived(*op)
            pass_on(*op)

    def fly(r, carry):
        for s in range(4):
            v = [zb[s, a, pl.ds(pl.multiple_of(r * 8, 8), 8), :] for a in range(16)]
            h = 1
            while h < 16:
                n = list(v)
                for a in range(16):
                    if a & h == 0:
                        n[a], n[a + h] = v[a] + v[a + h], v[a] - v[a + h]
                v = n
                h *= 2
            for a in range(16):
                z2[pl.ds(a * 1024 + r * 32 + s, 8, stride=4), :] = v[a]
        return carry

    lax.fori_loop(0, 32, fly, 0)

    stage = (sa0, sa1, sa2, sa3, sa4, sa5, sa6, sa7)
    lanes = lax.broadcasted_iota(I32, (8, 128), 1)
    sub = lax.broadcasted_iota(I32, (128, 128), 0)

    def fetch(t, base, n):
        for j in range(128):
            t[pl.ds(4 * j, 4), :] = z2[pl.ds(base[n, j], 4), :]

    def settle(t, i, n):
        h = jnp.where(parity(sub & lane_v[i, n:n + 1, :]) == 1, -1.0, 1.0).astype(BF16)
        hi, lo = halves(t[...])
        r = jnp.dot(
            jnp.concatenate([hi, lo], axis=1), jnp.concatenate([h, h], axis=0), preferred_element_type=F32
        )
        acc = [jnp.zeros((8, 128), F32) for _ in range(4)]
        for q in range(64):
            acc[q % 4] = jnp.where((lanes >> 1) == q, r[8 * q:8 * q + 8, :], acc[q % 4])
        t = (acc[0] + acc[1]) + (acc[2] + acc[3])
        t = jnp.where((lanes[:4] & 1) == 0, t[:4], t[4:])
        for s in range(4):
            ps[s, i, n:n + 1, :] = t[s:s + 1, :]

    def round_(new, index, base, m, old):
        index(m).wait()
        for n in range(4):
            fetch(new[n], base, n)
            if old is not None:
                settle(old[n], m - 1, n)
        index(jnp.minimum(m + 2, 15)).start()

    def pick(i, carry):
        round_(stage[4:], index_b, base_b, 2 * i + 1, stage[:4])
        round_(stage[:4], index_a, base_a, 2 * i + 2, stage[4:])
        return carry

    round_(stage[:4], index_a, base_a, 0, None)
    lax.fori_loop(0, 7, pick, 0)
    index_b(15).wait()
    for n in range(4):
        fetch(stage[4 + n], base_b, n)
        settle(stage[n], 14, n)
    for n in range(4):
        settle(stage[4 + n], 15, n)
    index_a(0).wait()

    big = jnp.broadcast_to(idall[2, 0:1, 0:1], (16, 4, 128))
    sign = sgn_v[...]
    for e in range(4):
        t = jnp.where(big > e, ps[min(e + 1, 3)], ps[e])
        t = jnp.where(big == e, ps[0], t) * sign
        for h in range(2):
            for i in range(4):
                pd[e * 2 + h, i, 0:4] = t[i * 4 + h * 2]
                pd[e * 2 + h, i, 4:8] = t[i * 4 + h * 2 + 1]
    me8 = d * 2 + zh
    r1[me8] = pd[me8]
    for n, (k, m) in enumerate(line):
        tz, tc = (z + k) % 4, (c + m) % 2
        dest = ((tz % 2) * 2 + tc) * 2 + tz // 2
        cp = remote(pd.at[dest], r1.at[me8], s1.at[n], w1.at[me8], mate(k, m))
        cp.start()
        pending.append(cp)
    for k, m in line:
        tz, tc = (z + k) % 4, (c + m) % 2
        src = ((tz % 2) * 2 + tc) * 2 + tz // 2
        remote(pd.at[src], r1.at[src], s1.at[0], w1.at[src], sibling).wait_recv()
    for i in range(4):
        t = r1[0, i]
        for n in range(1, 8):
            t = t + r1[n, i]
        for j in range(4):
            q2[i * 4 + j, 0:2, :] = t[2 * j:2 * j + 2, :]
            q2[i * 4 + j, 2:8, :] = jnp.zeros((6, 128), F32)
    r2[own] = q2[own]
    for n, (i, j) in enumerate(plane):
        dest = ((x + sig * i + 4) % 4) * 4 + (y + sig * j + 4) % 4
        cp = remote(q2.at[dest], r2.at[own], s2.at[n], w2.at[own], near(i, j))
        cp.start()
        pending.append(cp)
    for i, j in plane:
        src = ((x + sig * i + 4) % 4) * 4 + (y + sig * j + 4) % 4
        remote(q2.at[src], r2.at[src], s2.at[0], w2.at[src], sibling).wait_recv()
    t = r2[0]
    for n in range(1, 16):
        t = t + r2[n]
    out[...] = t

    @pl.when(c != zh)
    def _():
        near_x.wait_send()
        for cp in relays:
            cp.wait_send()

    x_side.wait_send()
    x_over.wait_send()
    for cp in pending:
        cp.wait_send()


def on_device(layer_input, output_grad, doc_ids, sign_bits, kept_rows, kept_cols):
    vm = pl.BlockSpec(memory_space=pltpu.VMEM)
    dma = pltpu.SemaphoreType.DMA
    scratch = [
        pltpu.VMEM((16, 4, 128), I32),
        pltpu.VMEM((16, 4, 128), I32),
        pltpu.VMEM((16, 4, 512, 128), BF16),
        pltpu.VMEM((4, 16, 256, 128), F32),
        pltpu.VMEM((16384, 128), F32),
        pltpu.VMEM((4, 512, 256), BF16),
        pltpu.VMEM((256, 1536), BF16),
        pltpu.VMEM((768, 512), BF16),
        pltpu.VMEM((16, 256, 128), BF16),
        pltpu.VMEM((16, 256, 128), I32),
        pltpu.VMEM((8, 256, 128), I32),
        pltpu.VMEM((8, 256, 128), BF16),
        pltpu.VMEM((4, 4, 128), I32),
        pltpu.VMEM((256, 256), BF16),
        pltpu.VMEM((512, 256), BF16),
        pltpu.VMEM((16, 4, 128), I32),
        pltpu.VMEM((16, 4, 128), I32),
        pltpu.VMEM((16, 4, 128), F32),
        pltpu.SMEM((4, 128), I32),
        pltpu.SMEM((4, 128), I32),
        pltpu.VMEM((512, 128), F32),
        pltpu.VMEM((512, 128), F32),
        pltpu.VMEM((512, 128), F32),
        pltpu.VMEM((512, 128), F32),
        pltpu.VMEM((512, 128), F32),
        pltpu.VMEM((512, 128), F32),
        pltpu.VMEM((512, 128), F32),
        pltpu.VMEM((512, 128), F32),
        pltpu.VMEM((4, 16, 4, 128), F32),
        pltpu.VMEM((8, 4, 8, 128), F32),
        pltpu.VMEM((8, 4, 8, 128), F32),
        pltpu.VMEM((16, 8, 128), F32),
        pltpu.VMEM((16, 8, 128), F32),
        dma((4,)), dma((31,)), dma((2, 4, 4)), dma((2, 4, 4)), dma((2, 4, 4)),
        dma((5,)), dma((4,)), dma(()), dma((3,)), dma((4,)),
        dma((8,)), dma((16,)), dma((8,)), dma((8, 2)), dma((2,)),
        dma((7,)), dma((8,)), dma((15,)), dma((16,)),
    ]
    got = pl.pallas_call(
        kernel,
        out_shape=jax.ShapeDtypeStruct((8, 128), F32),
        in_specs=[pl.BlockSpec(memory_space=pl.ANY)] * 6,
        out_specs=vm,
        scratch_shapes=scratch,
        compiler_params=pltpu.CompilerParams(
            collective_id=0, has_side_effects=True, vmem_limit_bytes=60 << 20
        ),
        name="sketch",
    )(
        layer_input, output_grad, doc_ids.reshape(4, 128), sign_bits,
        kept_rows.reshape(16, 4, 128), kept_cols.reshape(16, 4, 128),
    )
    return got[:2].reshape(1, 256)


def solution(mesh):
    placed = (P("doc", "param"), P("doc", "param"), P("doc"), P("param", None), P(), P())
    return jax.shard_map(
        on_device, mesh=mesh, in_specs=placed, out_specs=P("doc", "param"), check_vma=False
    )
```

```python
import functools

import jax
import jax.numpy as jnp
from jax import lax
from jax.experimental import pallas as pl
from jax.experimental.pallas import tpu as pltpu
from jax.sharding import PartitionSpec as P

MESH = pl.DeviceIdType.MESH
F32, BF16, I32 = jnp.float32, jnp.bfloat16, jnp.int32

PAIRS = [
    ((1, 0), (3, 0)), ((0, 1), (0, 3)), ((1, 1), (3, 3)), ((1, 3), (3, 1)),
    ((0, 0), (2, 0)), ((2, 1), (2, 3)), ((1, 2), (3, 2)), ((0, 2), (2, 2)),
]
OPS = [
    (1, 0, 0), (0, 1, 0), (0, 3, 0), "relay", (1, 0, 1), (1, 0, 3), "signs", (0, 2, 0), (1, 0, 2), (0, 0, 1),
    (1, 1, 0), (0, 1, 1), (1, 1, 1), (0, 3, 1), (1, 1, 3), (0, 0, 3), (1, 3, 0), "inputs", 0, 1, (0, 1, 3), (1, 3, 1),
    (0, 3, 3), (1, 3, 3), 2, 3, (0, 2, 1), (1, 1, 2), (0, 0, 2), (1, 2, 0), 4, (0, 2, 3), (1, 3, 2), (0, 1, 2),
    (0, 3, 2), 6, (1, 2, 1), (1, 2, 3), 5, (0, 2, 2), (1, 2, 2), 7,
]


def hops(piece, u, v):
    a, b = (u, v) if piece == 0 else (v, u)
    if (a, b) == (0, 0):
        out = [(1, 0), (3, 0), (0, 1), (0, 3)]
    elif b == 0:
        out = ([(1, 0)] if a == 1 else []) + [(0, 1), (0, 3)]
    elif b == 1:
        out = [(0, 1)]
    else:
        out = []
    return out if piece == 0 else [(d, c) for c, d in out]


def parity(t):
    for s in (8, 4):
        t = t ^ (t >> s)
    return (jnp.int32(0x6996) >> (t & 15)) & 1


def sylvester(n):
    i = lax.broadcasted_iota(I32, (n, n), 0)
    j = lax.broadcasted_iota(I32, (n, n), 1)
    return (1 - 2 * parity(i & j)).astype(F32).astype(BF16)


def halves(t):
    hi = t.astype(BF16)
    lo = (t - hi.astype(F32)).astype(BF16)
    return hi, lo


def kernel(
    li, og, ids, sb, kr, kc, out,
    kr_v, kc_v, gbuf, zb, z2, xq, xtb, xto, sg, stl, sts, sgs, idall, hm, mcol, lane_v, base_v, sgn_v, base_a, base_b,
    sa0, sa1, sa2, sa3, ps, pd, r1, q2, r2,
    lo_, gs, gr, ss, sr, xs_, xr, xl, ds_, dr, ls, lt, sgss, sgr, km, s1, w1, s2, w2,
):
    d = lax.axis_index("doc")
    p = lax.axis_index("param")
    x, zh, y = p // 8, (p // 4) % 2, p % 4
    zl, c = d // 2, d % 2
    z = zh * 2 + zl
    sig = 1 - 2 * c

    def dev(ax, ay, az, ac):
        return {"doc": (az % 2) * 2 + ac, "param": ax * 8 + (az // 2) * 4 + ay}

    def near(du, dv):
        return dev((x + sig * du + 4) % 4, (y + sig * dv + 4) % 4, z, c)

    sibling = dev(x, y, z, 1 - c)
    own = x * 4 + y

    bar = pltpu.get_barrier_semaphore()
    plane = [(i, j) for i in range(4) for j in range(4) if (i, j) != (0, 0)]
    ring = [(1, 0), (3, 0), (0, 1), (0, 3)]
    line = [(k, m) for k in range(4) for m in range(2) if (k, m) != (0, 0)]

    def mate(k, m):
        return dev(x, y, (z + k) % 4, (c + m) % 2)

    for i, j in ring:
        pl.semaphore_signal(bar, inc=1, device_id=near(i, j), device_id_type=MESH)
    for k, m in line:
        pl.semaphore_signal(bar, inc=1, device_id=mate(k, m), device_id_type=MESH)

    def half(l):
        return og.at[:, pl.ds(pl.multiple_of(l * 128, 128), 128)]

    own_g = pltpu.make_async_copy(half(zl), gbuf.at[own, d], lo_.at[0])
    own_i = pltpu.make_async_copy(ids, idall.at[d], lo_.at[1])
    own_r = pltpu.make_async_copy(kr, kr_v, lo_.at[2])
    own_c = pltpu.make_async_copy(kc, kc_v, lo_.at[3])
    for cp in (own_g, own_i, own_r, own_c):
        cp.start()

    def column(a, h, l):
        return pl.multiple_of(((a // 4) * 8 + h * 4 + a % 4) * 256 + l * 128, 128)

    def far_slot(u, v):
        f = 1 - 2 * zh
        return ((x - f * u + 4) % 4) * 4 + (y - f * v + 4) % 4

    sends = []
    for t in range(8):
        a = jnp.where(c == 0, far_slot(*PAIRS[t][0]), far_slot(*PAIRS[t][1]))
        cp = pltpu.make_async_copy(sb.at[:, pl.ds(column(a, 1 - zh, 1 - zl), 128)], sts.at[t], ls.at[t])
        cp.start()
        sends.append((a, cp))
    keeps = []
    for a in range(16):
        keeps.append(pltpu.make_async_copy(sb.at[:, pl.ds(column(a, zh, zl), 128)], stl.at[a], lt.at[a]))

    @pl.when(c == zh)
    def _():
        for cp in keeps:
            cp.start()

    pl.semaphore_wait(bar, len(ring) + len(line))

    def remote(src, dst, s, r, to):
        return pltpu.make_async_remote_copy(
            src_ref=src, dst_ref=dst, send_sem=s, recv_sem=r, device_id=to, device_id_type=MESH
        )

    pending = []
    count = [0]

    def quarter(piece):
        return (zl if piece == 0 else 1 - zl) * 2 + c

    def slot(u, v):
        return ((x - sig * u + 4) % 4) * 4 + (y - sig * v + 4) % 4

    def pass_on(piece, u, v):
        ref = gbuf.at[slot(u, v), quarter(piece)]
        src = half(zl) if (piece, u, v) == (0, 0, 0) else ref
        for du, dv in hops(piece, u, v):
            cp = remote(src, ref, gs.at[count[0]], gr.at[piece, (u + du) % 4, (v + dv) % 4], near(du, dv))
            count[0] += 1
            cp.start()
            pending.append(cp)
        cp = remote(src, ref, ss.at[piece, u, v], sr.at[piece, u, v], sibling)
        cp.start()
        pending.append(cp)

    def arrived(piece, u, v):
        ref = gbuf.at[slot(u, v), quarter(piece)]
        remote(ref, ref, ss.at[piece, u, v], gr.at[piece, u, v], sibling).wait_recv()

    ex = remote(
        half(1 - zl), gbuf.at[own, d], gs.at[30], gr.at[1, 0, 0],
        dev(x, y, zh * 2 + 1 - zl, c),
    )
    ex.start()
    pending.append(ex)
    pass_on(0, 0, 0)
    for i, to in enumerate([sibling, dev(x, y, zh * 2 + 1 - zl, c), dev(x, y, zh * 2 + 1 - zl, 1 - c)]):
        cp = remote(ids, idall.at[d], ds_.at[i], dr.at[d], to)
        cp.start()
        pending.append(cp)

    beside, across = zh * 2 + 1 - zl, (1 - zh) * 2 + 1 - zl
    x_over = remote(li, xq.at[d], xs_.at[2], xr.at[d], dev(x, y, across, zh))
    x_over.start()
    x_side = remote(li, xq.at[d], xs_.at[1], xr.at[d], dev(x, y, beside, zh))
    x_side.start()
    near_x = remote(li, xq.at[d], xs_.at[0], xr.at[d], sibling)
    own_x = pltpu.make_async_copy(li, xq.at[d], xl)

    @pl.when(c != zh)
    def _():
        near_x.start()

    @pl.when(c == zh)
    def _():
        own_x.start()

    relays = []
    for k in range(2):
        ref = xq.at[(1 - zl) * 2 + k]
        relays.append(remote(ref, ref, xs_.at[3 + k], xr.at[(1 - zl) * 2 + k], dev(x, y, beside, c)))

    for t in range(8):
        sends[t][1].wait()
        sgs[t] = (2 * sts[t] - 1).astype(F32).astype(BF16)

    def relay():
        for k in range(2):
            @pl.when(c != zh)
            def _():
                relays[k].wait_recv()
                relays[k].start()

    def send_signs():
        for t in range(8):
            cp = remote(sgs.at[t], sg.at[sends[t][0]], sgss.at[t], sgr.at[t, c], dev(x, y, across, zh))
            cp.start()
            pending.append(cp)


    @pl.when(c == zh)
    def _():
        for a in range(16):
            keeps[a].wait()
            sg[a] = (2 * stl[a] - 1).astype(F32).astype(BF16)

    own_r.wait()
    own_c.wait()
    rows, cols = kr_v[...], kc_v[...]
    base_v[...] = ((((cols >> 11) & 3) * 4 + ((cols >> 8) & 3)) * 256 + (rows & 255)) * 4
    lane_v[...] = cols & 127
    rmask = x * 2048 + c * 1024 + y * 256
    cmask = zh * 1024 + zl * 128
    bits = parity((rows & rmask) ^ (cols & cmask))
    sgn_v[...] = (1 - 2 * bits).astype(F32) * (1.0 / 8192)
    def index_a(i):
        return pltpu.make_async_copy(base_v.at[i], base_a, km.at[0])

    def index_b(i):
        return pltpu.make_async_copy(base_v.at[i], base_b, km.at[1])

    index_a(0).start()
    index_b(1).start()
    hm[...] = sylvester(256)

    def prepare():
        for q in range(4):
            got = remote(li, xq.at[q], xs_.at[0], xr.at[q], sibling)
            mine = (d == q) & (c == zh)
            seen = (c != zh) & ((q // 2) != zl)

            @pl.when(mine)
            def _():
                own_x.wait()

            @pl.when(jnp.logical_not(mine | seen))
            def _():
                got.wait_recv()

            @pl.when(d == q)
            def _():
                own_i.wait()

            @pl.when(d != q)
            def _():
                remote(ids, idall.at[q], ds_.at[0], dr.at[q], sibling).wait_recv()

        def labels(q):
            return jnp.concatenate([idall[q, i:i + 1, :] for i in range(4)], axis=1)

        big = idall[2, 0:1, 0:1]
        id0, id3 = labels(0), labels(3)
        short = id0 != big
        x0, x3 = xq[0].astype(F32).T, xq[3].astype(F32).T
        xtb[:, 0:512] = xq[1].astype(F32).T.astype(BF16)
        xtb[:, 512:1024] = xq[2].astype(F32).T.astype(BF16)
        xtb[:, 1024:1536] = jnp.where(short, x3, x0).astype(BF16)
        rest, id_rest = jnp.where(short, x0, x3), jnp.where(short, id0, id3)
        for o in range(3):
            label = o + (big <= o).astype(I32)
            xto[o * 256:(o + 1) * 256, :] = jnp.where(id_rest == label, rest, 0.0).astype(BF16)
        side = jnp.broadcast_to(short.astype(F32), (128, 512)).T.astype(BF16)
        mcol[...] = jnp.concatenate([side, side], axis=1)

    def pair(n):
        one, two = PAIRS[n]
        for u, v in (one, two):
            for piece in range(2):
                a, b = (-u) % 4, (-v) % 4
                qt = (zl if piece == 0 else 1 - zl) * 2 + 1 - c
                ref = gbuf.at[slot(u, v), qt]
                remote(ref, ref, ss.at[piece, a, b], sr.at[piece, a, b], sibling).wait_recv()
        sa, sb_ = slot(*one), slot(*two)

        @pl.when(c != zh)
        def _():
            for h, a in enumerate((sa, sb_)):
                remote(sgs.at[0], sg.at[a], sgss.at[0], sgr.at[n, h], sibling).wait_recv()

        w = [jnp.concatenate([gbuf[sa, q], gbuf[sb_, q]], axis=1) for q in range(4)]
        signs = jnp.concatenate([sg[sa], sg[sb_]], axis=1).astype(F32)
        short = mcol[...] != 0
        long_w = jnp.concatenate([w[1], w[2], jnp.where(short, w[3], w[0])], axis=0)
        g0 = jnp.dot(xtb[...], long_w, preferred_element_type=F32)
        g1 = jnp.dot(xto[...], jnp.where(short, w[0], w[3]), preferred_element_type=F32)
        for s in range(4):
            g = g0 if s == 0 else g1[(s - 1) * 256:s * 256]
            hi, lo = halves(g * signs)
            t = jnp.dot(hm[...], hi, preferred_element_type=F32) + jnp.dot(hm[...], lo, preferred_element_type=F32)
            zb[s, sa] = t[:, :128]
            zb[s, sb_] = t[:, 128:]

    own_g.wait()
    for op in OPS:
        if op == "signs":
            send_signs()
        elif op == "relay":
            relay()
        elif op == "inputs":
            prepare()
        elif isinstance(op, int):
            pair(op)
        else:
            arrived(*op)
            pass_on(*op)

    def fly(r, carry):
        for s in range(4):
            v = [zb[s, a, pl.ds(pl.multiple_of(r * 8, 8), 8), :] for a in range(16)]
            h = 1
            while h < 16:
                n = list(v)
                for a in range(16):
                    if a & h == 0:
                        n[a], n[a + h] = v[a] + v[a + h], v[a] - v[a + h]
                v = n
                h *= 2
            for a in range(16):
                z2[pl.ds(a * 1024 + r * 32 + s, 8, stride=4), :] = v[a]
        return carry

    lax.fori_loop(0, 32, fly, 0)

    stage = (sa0, sa1, sa2, sa3)
    lanes = lax.broadcasted_iota(I32, (8, 128), 1)
    sub = lax.broadcasted_iota(I32, (128, 128), 0)

    def fetch(t, base, n):
        for j in range(128):
            t[pl.ds(4 * j, 4), :] = z2[pl.ds(base[n, j], 4), :]

    def settle(ta, tb, i, n):
        h = jnp.concatenate(
            [jnp.where(parity(sub & lane_v[i, n + b:n + b + 1, :]) == 1, -1.0, 1.0).astype(BF16) for b in range(2)],
            axis=1,
        )
        both = [jnp.concatenate(halves(t[...]), axis=1) for t in (ta, tb)]
        r = jnp.dot(
            jnp.concatenate(both, axis=0), jnp.concatenate([h, h], axis=0), preferred_element_type=F32
        )
        for b in range(2):
            acc = [jnp.zeros((8, 128), F32) for _ in range(4)]
            for q in range(64):
                o = 512 * b + 8 * q
                acc[q % 4] = jnp.where((lanes >> 1) == q, r[o:o + 8, 128 * b:128 * b + 128], acc[q % 4])
            t = (acc[0] + acc[1]) + (acc[2] + acc[3])
            t = jnp.where((lanes[:4] & 1) == 0, t[:4], t[4:])
            for s in range(4):
                ps[s, i, n + b:n + b + 1, :] = t[s:s + 1, :]

    def pick(i, carry):
        for k, (index, base) in enumerate(((index_a, base_a), (index_b, base_b))):
            m = 2 * i + k
            index(m).wait()
            for n in range(4):
                fetch(stage[n], base, n)
            index(jnp.minimum(m + 2, 15)).start()
            settle(stage[0], stage[1], m, 0)
            settle(stage[2], stage[3], m, 2)
        return carry

    me8 = d * 2 + zh

    def emit(part):
        at = 8 * part
        big = jnp.broadcast_to(idall[2, 0:1, 0:1], (8, 4, 128))
        sign = sgn_v[at:at + 8]
        for e in range(4):
            t = jnp.where(big > e, ps[min(e + 1, 3), at:at + 8], ps[e, at:at + 8])
            t = jnp.where(big == e, ps[0, at:at + 8], t) * sign
            for h in range(2):
                for i in range(2):
                    pd[part, e * 2 + h, i, 0:4] = t[i * 4 + h * 2]
                    pd[part, e * 2 + h, i, 4:8] = t[i * 4 + h * 2 + 1]
        r1[part, me8] = pd[part, me8]
        for n, (k, m) in enumerate(line):
            tz, tc = (z + k) % 4, (c + m) % 2
            dest = ((tz % 2) * 2 + tc) * 2 + tz // 2
            cp = remote(pd.at[part, dest], r1.at[part, me8], s1.at[part, n], w1.at[part, me8], mate(k, m))
            cp.start()
            pending.append(cp)

    lax.fori_loop(0, 4, pick, 0)
    emit(0)
    lax.fori_loop(4, 8, pick, 0)
    emit(1)
    index_a(0).wait()
    index_b(0).wait()
    for part in range(2):
        for k, m in line:
            tz, tc = (z + k) % 4, (c + m) % 2
            src = ((tz % 2) * 2 + tc) * 2 + tz // 2
            remote(pd.at[part, src], r1.at[part, src], s1.at[part, 0], w1.at[part, src], sibling).wait_recv()
    for i in range(4):
        t = r1[i // 2, 0, i % 2]
        for n in range(1, 8):
            t = t + r1[i // 2, n, i % 2]
        for j in range(4):
            q2[i * 4 + j, 0:2, :] = t[2 * j:2 * j + 2, :]
            q2[i * 4 + j, 2:8, :] = jnp.zeros((6, 128), F32)
    r2[own] = q2[own]
    for n, (i, j) in enumerate(plane):
        dest = ((x + sig * i + 4) % 4) * 4 + (y + sig * j + 4) % 4
        cp = remote(q2.at[dest], r2.at[own], s2.at[n], w2.at[own], near(i, j))
        cp.start()
        pending.append(cp)
    for i, j in plane:
        src = ((x + sig * i + 4) % 4) * 4 + (y + sig * j + 4) % 4
        remote(q2.at[src], r2.at[src], s2.at[0], w2.at[src], sibling).wait_recv()
    t = r2[0]
    for n in range(1, 16):
        t = t + r2[n]
    out[...] = t

    @pl.when(c != zh)
    def _():
        near_x.wait_send()
        for cp in relays:
            cp.wait_send()

    x_side.wait_send()
    x_over.wait_send()
    for cp in pending:
        cp.wait_send()


def on_device(layer_input, output_grad, doc_ids, sign_bits, kept_rows, kept_cols):
    vm = pl.BlockSpec(memory_space=pltpu.VMEM)
    dma = pltpu.SemaphoreType.DMA
    scratch = [
        pltpu.VMEM((16, 4, 128), I32),
        pltpu.VMEM((16, 4, 128), I32),
        pltpu.VMEM((16, 4, 512, 128), BF16),
        pltpu.VMEM((4, 16, 256, 128), F32),
        pltpu.VMEM((16384, 128), F32),
        pltpu.VMEM((4, 512, 256), BF16),
        pltpu.VMEM((256, 1536), BF16),
        pltpu.VMEM((768, 512), BF16),
        pltpu.VMEM((16, 256, 128), BF16),
        pltpu.VMEM((16, 256, 128), I32),
        pltpu.VMEM((8, 256, 128), I32),
        pltpu.VMEM((8, 256, 128), BF16),
        pltpu.VMEM((4, 4, 128), I32),
        pltpu.VMEM((256, 256), BF16),
        pltpu.VMEM((512, 256), BF16),
        pltpu.VMEM((16, 4, 128), I32),
        pltpu.VMEM((16, 4, 128), I32),
        pltpu.VMEM((16, 4, 128), F32),
        pltpu.SMEM((4, 128), I32),
        pltpu.SMEM((4, 128), I32),
        pltpu.VMEM((512, 128), F32),
        pltpu.VMEM((512, 128), F32),
        pltpu.VMEM((512, 128), F32),
        pltpu.VMEM((512, 128), F32),
        pltpu.VMEM((4, 16, 4, 128), F32),
        pltpu.VMEM((2, 8, 2, 8, 128), F32),
        pltpu.VMEM((2, 8, 2, 8, 128), F32),
        pltpu.VMEM((16, 8, 128), F32),
        pltpu.VMEM((16, 8, 128), F32),
        dma((4,)), dma((31,)), dma((2, 4, 4)), dma((2, 4, 4)), dma((2, 4, 4)),
        dma((5,)), dma((4,)), dma(()), dma((3,)), dma((4,)),
        dma((8,)), dma((16,)), dma((8,)), dma((8, 2)), dma((2,)),
        dma((2, 7)), dma((2, 8)), dma((15,)), dma((16,)),
    ]
    got = pl.pallas_call(
        kernel,
        out_shape=jax.ShapeDtypeStruct((8, 128), F32),
        in_specs=[pl.BlockSpec(memory_space=pl.ANY)] * 6,
        out_specs=vm,
        scratch_shapes=scratch,
        compiler_params=pltpu.CompilerParams(
            collective_id=0, has_side_effects=True, vmem_limit_bytes=60 << 20
        ),
        name="sketch",
    )(
        layer_input, output_grad, doc_ids.reshape(4, 128), sign_bits,
        kept_rows.reshape(16, 4, 128), kept_cols.reshape(16, 4, 128),
    )
    return got[:2].reshape(1, 256)


def solution(mesh):
    placed = (P("doc", "param"), P("doc", "param"), P("doc"), P("param", None), P(), P())
    return jax.shard_map(
        on_device, mesh=mesh, in_specs=placed, out_specs=P("doc", "param"), check_vma=False
    )
```

```python
import functools

import jax
import jax.numpy as jnp
from jax import lax
from jax.experimental import pallas as pl
from jax.experimental.pallas import tpu as pltpu
from jax.sharding import PartitionSpec as P

MESH = pl.DeviceIdType.MESH
F32, BF16, I32 = jnp.float32, jnp.bfloat16, jnp.int32

PAIRS = [
    ((1, 0), (3, 0)), ((0, 1), (0, 3)), ((1, 1), (3, 3)), ((1, 3), (3, 1)),
    ((0, 0), (2, 0)), ((2, 1), (2, 3)), ((1, 2), (3, 2)), ((0, 2), (2, 2)),
]
OPS = [
    (1, 0, 0), (0, 1, 0), (0, 3, 0), "relay", (1, 0, 1), (1, 0, 3), "signs", (0, 2, 0), (1, 0, 2), (0, 0, 1),
    (1, 1, 0), (0, 1, 1), (1, 1, 1), (0, 3, 1), (1, 1, 3), (0, 0, 3), (1, 3, 0), (0, 1, 3), (1, 3, 1), (0, 3, 3),
    (1, 3, 3), "inputs", 0, (0, 2, 1), (1, 1, 2), 1, (0, 0, 2), (1, 2, 0), 2, (0, 2, 3), (1, 3, 2), 3, (0, 1, 2),
    (0, 3, 2), 4, (1, 2, 1), (1, 2, 3), 6, (0, 2, 2), (1, 2, 2), 5, 7,
]


def hops(piece, u, v):
    a, b = (u, v) if piece == 0 else (v, u)
    if (a, b) == (0, 0):
        out = [(1, 0), (3, 0), (0, 1), (0, 3)]
    elif b == 0:
        out = ([(1, 0)] if a == 1 else []) + [(0, 1), (0, 3)]
    elif b == 1:
        out = [(0, 1)]
    else:
        out = []
    return out if piece == 0 else [(d, c) for c, d in out]


def parity(t):
    for s in (8, 4):
        t = t ^ (t >> s)
    return (jnp.int32(0x6996) >> (t & 15)) & 1


def sylvester(n):
    i = lax.broadcasted_iota(I32, (n, n), 0)
    j = lax.broadcasted_iota(I32, (n, n), 1)
    return (1 - 2 * parity(i & j)).astype(F32).astype(BF16)


def halves(t):
    hi = t.astype(BF16)
    lo = (t - hi.astype(F32)).astype(BF16)
    return hi, lo


def kernel(
    li, og, ids, sb, kr, kc, out,
    kr_v, kc_v, gbuf, zb, z2, xq, xtb, xto, sg, stl, sts, sgs, idall, hm, mcol, lane_v, base_v, sgn_v, base_a, base_b,
    sa0, sa1, sa2, sa3, ps, pd, r1, q2, r2,
    lo_, gs, gr, ss, sr, xs_, xr, xl, ds_, dr, ls, lt, sgss, sgr, km, s1, w1, s2, w2,
):
    d = lax.axis_index("doc")
    p = lax.axis_index("param")
    x, zh, y = p // 8, (p // 4) % 2, p % 4
    zl, c = d // 2, d % 2
    z = zh * 2 + zl
    sig = 1 - 2 * c

    def dev(ax, ay, az, ac):
        return {"doc": (az % 2) * 2 + ac, "param": ax * 8 + (az // 2) * 4 + ay}

    def near(du, dv):
        return dev((x + sig * du + 4) % 4, (y + sig * dv + 4) % 4, z, c)

    sibling = dev(x, y, z, 1 - c)
    own = x * 4 + y

    bar = pltpu.get_barrier_semaphore()
    plane = [(i, j) for i in range(4) for j in range(4) if (i, j) != (0, 0)]
    ring = [(1, 0), (3, 0), (0, 1), (0, 3)]
    line = [(k, m) for k in range(4) for m in range(2) if (k, m) != (0, 0)]

    def mate(k, m):
        return dev(x, y, (z + k) % 4, (c + m) % 2)

    for i, j in ring:
        pl.semaphore_signal(bar, inc=1, device_id=near(i, j), device_id_type=MESH)
    for k, m in line:
        pl.semaphore_signal(bar, inc=1, device_id=mate(k, m), device_id_type=MESH)

    def half(l):
        return og.at[:, pl.ds(pl.multiple_of(l * 128, 128), 128)]

    own_g = pltpu.make_async_copy(half(zl), gbuf.at[own, d], lo_.at[0])
    own_i = pltpu.make_async_copy(ids, idall.at[d], lo_.at[1])
    own_r = pltpu.make_async_copy(kr, kr_v, lo_.at[2])
    own_c = pltpu.make_async_copy(kc, kc_v, lo_.at[3])
    for cp in (own_g, own_i, own_r, own_c):
        cp.start()

    def column(a, h, l):
        return pl.multiple_of(((a // 4) * 8 + h * 4 + a % 4) * 256 + l * 128, 128)

    def far_slot(u, v):
        f = 1 - 2 * zh
        return ((x - f * u + 4) % 4) * 4 + (y - f * v + 4) % 4

    sends = []
    for t in range(8):
        a = jnp.where(c == 0, far_slot(*PAIRS[t][0]), far_slot(*PAIRS[t][1]))
        cp = pltpu.make_async_copy(sb.at[:, pl.ds(column(a, 1 - zh, 1 - zl), 128)], sts.at[t], ls.at[t])
        cp.start()
        sends.append((a, cp))
    keeps = []
    for a in range(16):
        keeps.append(pltpu.make_async_copy(sb.at[:, pl.ds(column(a, zh, zl), 128)], stl.at[a], lt.at[a]))

    @pl.when(c == zh)
    def _():
        for cp in keeps:
            cp.start()

    pl.semaphore_wait(bar, len(ring) + len(line))

    def remote(src, dst, s, r, to):
        return pltpu.make_async_remote_copy(
            src_ref=src, dst_ref=dst, send_sem=s, recv_sem=r, device_id=to, device_id_type=MESH
        )

    pending = []
    count = [0]

    def quarter(piece):
        return (zl if piece == 0 else 1 - zl) * 2 + c

    def slot(u, v):
        return ((x - sig * u + 4) % 4) * 4 + (y - sig * v + 4) % 4

    def pass_on(piece, u, v):
        ref = gbuf.at[slot(u, v), quarter(piece)]
        src = half(zl) if (piece, u, v) == (0, 0, 0) else ref
        for du, dv in hops(piece, u, v):
            cp = remote(src, ref, gs.at[count[0]], gr.at[piece, (u + du) % 4, (v + dv) % 4], near(du, dv))
            count[0] += 1
            cp.start()
            pending.append(cp)
        cp = remote(src, ref, ss.at[piece, u, v], sr.at[piece, u, v], sibling)
        cp.start()
        pending.append(cp)

    def arrived(piece, u, v):
        ref = gbuf.at[slot(u, v), quarter(piece)]
        remote(ref, ref, ss.at[piece, u, v], gr.at[piece, u, v], sibling).wait_recv()

    ex = remote(
        half(1 - zl), gbuf.at[own, d], gs.at[30], gr.at[1, 0, 0],
        dev(x, y, zh * 2 + 1 - zl, c),
    )
    ex.start()
    pending.append(ex)
    pass_on(0, 0, 0)
    for i, to in enumerate([sibling, dev(x, y, zh * 2 + 1 - zl, c), dev(x, y, zh * 2 + 1 - zl, 1 - c)]):
        cp = remote(ids, idall.at[d], ds_.at[i], dr.at[d], to)
        cp.start()
        pending.append(cp)

    beside, across = zh * 2 + 1 - zl, (1 - zh) * 2 + 1 - zl
    x_over = remote(li, xq.at[d], xs_.at[2], xr.at[d], dev(x, y, across, zh))
    x_over.start()
    x_side = remote(li, xq.at[d], xs_.at[1], xr.at[d], dev(x, y, beside, zh))
    x_side.start()
    near_x = remote(li, xq.at[d], xs_.at[0], xr.at[d], sibling)
    own_x = pltpu.make_async_copy(li, xq.at[d], xl)

    @pl.when(c != zh)
    def _():
        near_x.start()

    @pl.when(c == zh)
    def _():
        own_x.start()

    relays = []
    for k in range(2):
        ref = xq.at[(1 - zl) * 2 + k]
        relays.append(remote(ref, ref, xs_.at[3 + k], xr.at[(1 - zl) * 2 + k], dev(x, y, beside, c)))

    for t in range(8):
        sends[t][1].wait()
        sgs[t] = (2 * sts[t] - 1).astype(F32).astype(BF16)

    def relay():
        for k in range(2):
            @pl.when(c != zh)
            def _():
                relays[k].wait_recv()
                relays[k].start()

    def send_signs():
        for t in range(8):
            cp = remote(sgs.at[t], sg.at[sends[t][0]], sgss.at[t], sgr.at[t, c], dev(x, y, across, zh))
            cp.start()
            pending.append(cp)


    @pl.when(c == zh)
    def _():
        for a in range(16):
            keeps[a].wait()
            sg[a] = (2 * stl[a] - 1).astype(F32).astype(BF16)

    own_r.wait()
    own_c.wait()
    rows, cols = kr_v[...], kc_v[...]
    base_v[...] = ((((cols >> 11) & 3) * 4 + ((cols >> 8) & 3)) * 256 + (rows & 255)) * 4
    lane_v[...] = cols & 127
    rmask = x * 2048 + c * 1024 + y * 256
    cmask = zh * 1024 + zl * 128
    bits = parity((rows & rmask) ^ (cols & cmask))
    sgn_v[...] = (1 - 2 * bits).astype(F32) * (1.0 / 8192)
    def index_a(i):
        return pltpu.make_async_copy(base_v.at[i], base_a, km.at[0])

    def index_b(i):
        return pltpu.make_async_copy(base_v.at[i], base_b, km.at[1])

    index_a(0).start()
    index_b(1).start()
    hm[...] = sylvester(256)

    def prepare():
        for q in range(4):
            got = remote(li, xq.at[q], xs_.at[0], xr.at[q], sibling)
            mine = (d == q) & (c == zh)
            seen = (c != zh) & ((q // 2) != zl)

            @pl.when(mine)
            def _():
                own_x.wait()

            @pl.when(jnp.logical_not(mine | seen))
            def _():
                got.wait_recv()

            @pl.when(d == q)
            def _():
                own_i.wait()

            @pl.when(d != q)
            def _():
                remote(ids, idall.at[q], ds_.at[0], dr.at[q], sibling).wait_recv()

        def labels(q):
            return jnp.concatenate([idall[q, i:i + 1, :] for i in range(4)], axis=1)

        big = idall[2, 0:1, 0:1]
        id0, id3 = labels(0), labels(3)
        short = id0 != big
        x0, x3 = xq[0].astype(F32).T, xq[3].astype(F32).T
        xtb[:, 0:512] = xq[1].astype(F32).T.astype(BF16)
        xtb[:, 512:1024] = xq[2].astype(F32).T.astype(BF16)
        xtb[:, 1024:1536] = jnp.where(short, x3, x0).astype(BF16)
        rest, id_rest = jnp.where(short, x0, x3), jnp.where(short, id0, id3)
        for o in range(3):
            label = o + (big <= o).astype(I32)
            xto[o * 256:(o + 1) * 256, :] = jnp.where(id_rest == label, rest, 0.0).astype(BF16)
        side = jnp.broadcast_to(short.astype(F32), (128, 512)).T.astype(BF16)
        mcol[...] = jnp.concatenate([side, side], axis=1)

    def pair(n):
        one, two = PAIRS[n]
        for u, v in (one, two):
            for piece in range(2):
                a, b = (-u) % 4, (-v) % 4
                qt = (zl if piece == 0 else 1 - zl) * 2 + 1 - c
                ref = gbuf.at[slot(u, v), qt]
                remote(ref, ref, ss.at[piece, a, b], sr.at[piece, a, b], sibling).wait_recv()
        sa, sb_ = slot(*one), slot(*two)

        @pl.when(c != zh)
        def _():
            for h, a in enumerate((sa, sb_)):
                remote(sgs.at[0], sg.at[a], sgss.at[0], sgr.at[n, h], sibling).wait_recv()

        w = [jnp.concatenate([gbuf[sa, q], gbuf[sb_, q]], axis=1) for q in range(4)]
        signs = jnp.concatenate([sg[sa], sg[sb_]], axis=1).astype(F32)
        short = mcol[...] != 0
        long_w = jnp.concatenate([w[1], w[2], jnp.where(short, w[3], w[0])], axis=0)
        g0 = jnp.dot(xtb[...], long_w, preferred_element_type=F32)
        g1 = jnp.dot(xto[...], jnp.where(short, w[0], w[3]), preferred_element_type=F32)
        for s in range(4):
            g = g0 if s == 0 else g1[(s - 1) * 256:s * 256]
            hi, lo = halves(g * signs)
            t = jnp.dot(hm[...], hi, preferred_element_type=F32) + jnp.dot(hm[...], lo, preferred_element_type=F32)
            zb[s, sa] = t[:, :128]
            zb[s, sb_] = t[:, 128:]

    own_g.wait()
    for op in OPS:
        if op == "signs":
            send_signs()
        elif op == "relay":
            relay()
        elif op == "inputs":
            prepare()
        elif isinstance(op, int):
            pair(op)
        else:
            arrived(*op)
            pass_on(*op)

    def fly(r, carry):
        for s in range(4):
            v = [zb[s, a, pl.ds(pl.multiple_of(r * 8, 8), 8), :] for a in range(16)]
            h = 1
            while h < 16:
                n = list(v)
                for a in range(16):
                    if a & h == 0:
                        n[a], n[a + h] = v[a] + v[a + h], v[a] - v[a + h]
                v = n
                h *= 2
            for a in range(16):
                z2[pl.ds(a * 1024 + r * 32 + s, 8, stride=4), :] = v[a]
        return carry

    lax.fori_loop(0, 32, fly, 0)

    stage = (sa0, sa1, sa2, sa3)
    lanes = lax.broadcasted_iota(I32, (8, 128), 1)
    sub = lax.broadcasted_iota(I32, (128, 128), 0)

    def fetch(t, base, n):
        for j in range(128):
            t[pl.ds(4 * j, 4), :] = z2[pl.ds(base[n, j], 4), :]

    def settle(ta, tb, i, n):
        h = jnp.concatenate(
            [jnp.where(parity(sub & lane_v[i, n + b:n + b + 1, :]) == 1, -1.0, 1.0).astype(BF16) for b in range(2)],
            axis=1,
        )
        both = [jnp.concatenate(halves(t[...]), axis=1) for t in (ta, tb)]
        r = jnp.dot(
            jnp.concatenate(both, axis=0), jnp.concatenate([h, h], axis=0), preferred_element_type=F32
        )
        for b in range(2):
            acc = [jnp.zeros((8, 128), F32) for _ in range(4)]
            for q in range(64):
                o = 512 * b + 8 * q
                acc[q % 4] = jnp.where((lanes >> 1) == q, r[o:o + 8, 128 * b:128 * b + 128], acc[q % 4])
            t = (acc[0] + acc[1]) + (acc[2] + acc[3])
            t = jnp.where((lanes[:4] & 1) == 0, t[:4], t[4:])
            for s in range(4):
                ps[s, i, n + b:n + b + 1, :] = t[s:s + 1, :]

    def pick(i, carry):
        for k, (index, base) in enumerate(((index_a, base_a), (index_b, base_b))):
            m = 2 * i + k
            index(m).wait()
            for n in range(4):
                fetch(stage[n], base, n)
            index(jnp.minimum(m + 2, 15)).start()
            settle(stage[0], stage[1], m, 0)
            settle(stage[2], stage[3], m, 2)
        return carry

    me8 = d * 2 + zh

    def emit(part):
        at = 8 * part
        big = jnp.broadcast_to(idall[2, 0:1, 0:1], (8, 4, 128))
        sign = sgn_v[at:at + 8]
        for e in range(4):
            t = jnp.where(big > e, ps[min(e + 1, 3), at:at + 8], ps[e, at:at + 8])
            t = jnp.where(big == e, ps[0, at:at + 8], t) * sign
            for h in range(2):
                for i in range(2):
                    pd[part, e * 2 + h, i, 0:4] = t[i * 4 + h * 2]
                    pd[part, e * 2 + h, i, 4:8] = t[i * 4 + h * 2 + 1]
        r1[part, me8] = pd[part, me8]
        for n, (k, m) in enumerate(line):
            tz, tc = (z + k) % 4, (c + m) % 2
            dest = ((tz % 2) * 2 + tc) * 2 + tz // 2
            cp = remote(pd.at[part, dest], r1.at[part, me8], s1.at[part, n], w1.at[part, me8], mate(k, m))
            cp.start()
            pending.append(cp)

    lax.fori_loop(0, 4, pick, 0)
    emit(0)
    lax.fori_loop(4, 8, pick, 0)
    emit(1)
    index_a(0).wait()
    index_b(0).wait()
    for part in range(2):
        for k, m in line:
            tz, tc = (z + k) % 4, (c + m) % 2
            src = ((tz % 2) * 2 + tc) * 2 + tz // 2
            remote(pd.at[part, src], r1.at[part, src], s1.at[part, 0], w1.at[part, src], sibling).wait_recv()
    for i in range(4):
        t = r1[i // 2, 0, i % 2]
        for n in range(1, 8):
            t = t + r1[i // 2, n, i % 2]
        for j in range(4):
            q2[i * 4 + j, 0:2, :] = t[2 * j:2 * j + 2, :]
            q2[i * 4 + j, 2:8, :] = jnp.zeros((6, 128), F32)
    r2[own] = q2[own]
    for n, (i, j) in enumerate(plane):
        dest = ((x + sig * i + 4) % 4) * 4 + (y + sig * j + 4) % 4
        cp = remote(q2.at[dest], r2.at[own], s2.at[n], w2.at[own], near(i, j))
        cp.start()
        pending.append(cp)
    for i, j in plane:
        src = ((x + sig * i + 4) % 4) * 4 + (y + sig * j + 4) % 4
        remote(q2.at[src], r2.at[src], s2.at[0], w2.at[src], sibling).wait_recv()
    t = r2[0]
    for n in range(1, 16):
        t = t + r2[n]
    out[...] = t

    @pl.when(c != zh)
    def _():
        near_x.wait_send()
        for cp in relays:
            cp.wait_send()

    x_side.wait_send()
    x_over.wait_send()
    for cp in pending:
        cp.wait_send()


def on_device(layer_input, output_grad, doc_ids, sign_bits, kept_rows, kept_cols):
    vm = pl.BlockSpec(memory_space=pltpu.VMEM)
    dma = pltpu.SemaphoreType.DMA
    scratch = [
        pltpu.VMEM((16, 4, 128), I32),
        pltpu.VMEM((16, 4, 128), I32),
        pltpu.VMEM((16, 4, 512, 128), BF16),
        pltpu.VMEM((4, 16, 256, 128), F32),
        pltpu.VMEM((16384, 128), F32),
        pltpu.VMEM((4, 512, 256), BF16),
        pltpu.VMEM((256, 1536), BF16),
        pltpu.VMEM((768, 512), BF16),
        pltpu.VMEM((16, 256, 128), BF16),
        pltpu.VMEM((16, 256, 128), I32),
        pltpu.VMEM((8, 256, 128), I32),
        pltpu.VMEM((8, 256, 128), BF16),
        pltpu.VMEM((4, 4, 128), I32),
        pltpu.VMEM((256, 256), BF16),
        pltpu.VMEM((512, 256), BF16),
        pltpu.VMEM((16, 4, 128), I32),
        pltpu.VMEM((16, 4, 128), I32),
        pltpu.VMEM((16, 4, 128), F32),
        pltpu.SMEM((4, 128), I32),
        pltpu.SMEM((4, 128), I32),
        pltpu.VMEM((512, 128), F32),
        pltpu.VMEM((512, 128), F32),
        pltpu.VMEM((512, 128), F32),
        pltpu.VMEM((512, 128), F32),
        pltpu.VMEM((4, 16, 4, 128), F32),
        pltpu.VMEM((2, 8, 2, 8, 128), F32),
        pltpu.VMEM((2, 8, 2, 8, 128), F32),
        pltpu.VMEM((16, 8, 128), F32),
        pltpu.VMEM((16, 8, 128), F32),
        dma((4,)), dma((31,)), dma((2, 4, 4)), dma((2, 4, 4)), dma((2, 4, 4)),
        dma((5,)), dma((4,)), dma(()), dma((3,)), dma((4,)),
        dma((8,)), dma((16,)), dma((8,)), dma((8, 2)), dma((2,)),
        dma((2, 7)), dma((2, 8)), dma((15,)), dma((16,)),
    ]
    got = pl.pallas_call(
        kernel,
        out_shape=jax.ShapeDtypeStruct((8, 128), F32),
        in_specs=[pl.BlockSpec(memory_space=pl.ANY)] * 6,
        out_specs=vm,
        scratch_shapes=scratch,
        compiler_params=pltpu.CompilerParams(
            collective_id=0, has_side_effects=True, vmem_limit_bytes=60 << 20
        ),
        name="sketch",
    )(
        layer_input, output_grad, doc_ids.reshape(4, 128), sign_bits,
        kept_rows.reshape(16, 4, 128), kept_cols.reshape(16, 4, 128),
    )
    return got[:2].reshape(1, 256)


def solution(mesh):
    placed = (P("doc", "param"), P("doc", "param"), P("doc"), P("param", None), P(), P())
    return jax.shard_map(
        on_device, mesh=mesh, in_specs=placed, out_specs=P("doc", "param"), check_vma=False
    )
```

```python
import functools

import jax
import jax.numpy as jnp
from jax import lax
from jax.experimental import pallas as pl
from jax.experimental.pallas import tpu as pltpu
from jax.sharding import PartitionSpec as P

MESH = pl.DeviceIdType.MESH
F32, BF16, I32 = jnp.float32, jnp.bfloat16, jnp.int32

PAIRS = [
    ((1, 0), (3, 0)), ((0, 1), (0, 3)), ((1, 1), (3, 3)), ((1, 3), (3, 1)),
    ((0, 0), (2, 0)), ((2, 1), (2, 3)), ((1, 2), (3, 2)), ((0, 2), (2, 2)),
]
OPS = [
    (1, 0, 0), (0, 1, 0), (0, 3, 0), "relay", (1, 0, 1), (1, 0, 3), "signs", (0, 2, 0), (1, 0, 2), (0, 0, 1),
    (1, 1, 0), (0, 1, 1), (1, 1, 1), (0, 3, 1), (1, 1, 3), (0, 0, 3), (1, 3, 0), (0, 1, 3), (1, 3, 1), (0, 3, 3),
    (1, 3, 3), "inputs", 0, (0, 2, 1), (1, 1, 2), 1, (0, 0, 2), (1, 2, 0), 2, (0, 2, 3), (1, 3, 2), 3, (0, 1, 2),
    (0, 3, 2), 4, (1, 2, 1), (1, 2, 3), 6, (0, 2, 2), (1, 2, 2), 5, 7,
]


def hops(piece, u, v):
    a, b = (u, v) if piece == 0 else (v, u)
    if (a, b) == (0, 0):
        out = [(1, 0), (3, 0), (0, 1), (0, 3)]
    elif b == 0:
        out = ([(1, 0)] if a == 1 else []) + [(0, 1), (0, 3)]
    elif b == 1:
        out = [(0, 1)]
    else:
        out = []
    return out if piece == 0 else [(d, c) for c, d in out]


def parity(t):
    for s in (8, 4):
        t = t ^ (t >> s)
    return (jnp.int32(0x6996) >> (t & 15)) & 1


def sylvester(n):
    i = lax.broadcasted_iota(I32, (n, n), 0)
    j = lax.broadcasted_iota(I32, (n, n), 1)
    return (1 - 2 * parity(i & j)).astype(F32).astype(BF16)


def halves(t):
    hi = t.astype(BF16)
    lo = (t - hi.astype(F32)).astype(BF16)
    return hi, lo


def kernel(
    li, og, ids, sb, kr, kc, out,
    kr_v, kc_v, gbuf, zb, z2, xq, xtb, xto, sg, stl, sts, sgs, idall, hm, mcol, lane_v, base_v, sgn_v, base_a, base_b,
    sa0, sa1, sa2, sa3, ps, pd, r1, q2, r2,
    lo_, gs, gr, ss, sr, xs_, xr, xl, ds_, dr, ls, lt, sgss, sgr, km, s1, w1, s2, w2,
):
    d = lax.axis_index("doc")
    p = lax.axis_index("param")
    x, zh, y = p // 8, (p // 4) % 2, p % 4
    zl, c = d // 2, d % 2
    z = zh * 2 + zl
    sig = 1 - 2 * c

    def dev(ax, ay, az, ac):
        return {"doc": (az % 2) * 2 + ac, "param": ax * 8 + (az // 2) * 4 + ay}

    def near(du, dv):
        return dev((x + sig * du + 4) % 4, (y + sig * dv + 4) % 4, z, c)

    sibling = dev(x, y, z, 1 - c)
    own = x * 4 + y

    bar = pltpu.get_barrier_semaphore()
    plane = [(i, j) for i in range(4) for j in range(4) if (i, j) != (0, 0)]
    ring = [(1, 0), (3, 0), (0, 1), (0, 3)]
    line = [(k, m) for k in range(4) for m in range(2) if (k, m) != (0, 0)]

    def mate(k, m):
        return dev(x, y, (z + k) % 4, (c + m) % 2)

    for i, j in ring:
        pl.semaphore_signal(bar, inc=1, device_id=near(i, j), device_id_type=MESH)
    for k, m in line:
        pl.semaphore_signal(bar, inc=1, device_id=mate(k, m), device_id_type=MESH)

    def half(l):
        return og.at[:, pl.ds(pl.multiple_of(l * 128, 128), 128)]

    own_g = pltpu.make_async_copy(half(zl), gbuf.at[own, d], lo_.at[0])
    own_i = pltpu.make_async_copy(ids, idall.at[d], lo_.at[1])
    own_r = pltpu.make_async_copy(kr, kr_v, lo_.at[2])
    own_c = pltpu.make_async_copy(kc, kc_v, lo_.at[3])
    for cp in (own_g, own_i, own_r, own_c):
        cp.start()

    def column(a, h, l):
        return pl.multiple_of(((a // 4) * 8 + h * 4 + a % 4) * 256 + l * 128, 128)

    def far_slot(u, v):
        f = 1 - 2 * zh
        return ((x - f * u + 4) % 4) * 4 + (y - f * v + 4) % 4

    sends = []
    for t in range(8):
        a = jnp.where(c == 0, far_slot(*PAIRS[t][0]), far_slot(*PAIRS[t][1]))
        cp = pltpu.make_async_copy(sb.at[:, pl.ds(column(a, 1 - zh, 1 - zl), 128)], sts.at[t], ls.at[t])
        cp.start()
        sends.append((a, cp))
    keeps = []
    for a in range(16):
        keeps.append(pltpu.make_async_copy(sb.at[:, pl.ds(column(a, zh, zl), 128)], stl.at[a], lt.at[a]))

    pl.semaphore_wait(bar, len(ring) + len(line))

    def remote(src, dst, s, r, to):
        return pltpu.make_async_remote_copy(
            src_ref=src, dst_ref=dst, send_sem=s, recv_sem=r, device_id=to, device_id_type=MESH
        )

    pending = []
    count = [0]

    def quarter(piece):
        return (zl if piece == 0 else 1 - zl) * 2 + c

    def slot(u, v):
        return ((x - sig * u + 4) % 4) * 4 + (y - sig * v + 4) % 4

    def pass_on(piece, u, v):
        ref = gbuf.at[slot(u, v), quarter(piece)]
        src = half(zl) if (piece, u, v) == (0, 0, 0) else ref
        for du, dv in hops(piece, u, v):
            cp = remote(src, ref, gs.at[count[0]], gr.at[piece, (u + du) % 4, (v + dv) % 4], near(du, dv))
            count[0] += 1
            cp.start()
            pending.append(cp)
        cp = remote(src, ref, ss.at[piece, u, v], sr.at[piece, u, v], sibling)
        cp.start()
        pending.append(cp)

    def arrived(piece, u, v):
        ref = gbuf.at[slot(u, v), quarter(piece)]
        remote(ref, ref, ss.at[piece, u, v], gr.at[piece, u, v], sibling).wait_recv()

    ex = remote(
        half(1 - zl), gbuf.at[own, d], gs.at[30], gr.at[1, 0, 0],
        dev(x, y, zh * 2 + 1 - zl, c),
    )
    ex.start()
    pending.append(ex)
    pass_on(0, 0, 0)
    for i, to in enumerate([sibling, dev(x, y, zh * 2 + 1 - zl, c), dev(x, y, zh * 2 + 1 - zl, 1 - c)]):
        cp = remote(ids, idall.at[d], ds_.at[i], dr.at[d], to)
        cp.start()
        pending.append(cp)

    beside, across = zh * 2 + 1 - zl, (1 - zh) * 2 + 1 - zl
    x_over = remote(li, xq.at[d], xs_.at[2], xr.at[d], dev(x, y, across, zh))
    x_over.start()
    x_side = remote(li, xq.at[d], xs_.at[1], xr.at[d], dev(x, y, beside, zh))
    x_side.start()
    near_x = remote(li, xq.at[d], xs_.at[0], xr.at[d], sibling)
    own_x = pltpu.make_async_copy(li, xq.at[d], xl)

    @pl.when(c != zh)
    def _():
        near_x.start()

    @pl.when(c == zh)
    def _():
        own_x.start()

    @pl.when(c == zh)
    def _():
        for cp in keeps:
            cp.start()

    relays = []
    for k in range(2):
        ref = xq.at[(1 - zl) * 2 + k]
        relays.append(remote(ref, ref, xs_.at[3 + k], xr.at[(1 - zl) * 2 + k], dev(x, y, beside, c)))

    for t in range(8):
        sends[t][1].wait()
        sgs[t] = (2 * sts[t] - 1).astype(F32).astype(BF16)

    def relay():
        for k in range(2):
            @pl.when(c != zh)
            def _():
                relays[k].wait_recv()
                relays[k].start()

    def send_signs():
        for t in range(8):
            cp = remote(sgs.at[t], sg.at[sends[t][0]], sgss.at[t], sgr.at[t, c], dev(x, y, across, zh))
            cp.start()
            pending.append(cp)


    @pl.when(c == zh)
    def _():
        for a in range(16):
            keeps[a].wait()
            sg[a] = (2 * stl[a] - 1).astype(F32).astype(BF16)

    own_r.wait()
    own_c.wait()
    rows, cols = kr_v[...], kc_v[...]
    base_v[...] = ((((cols >> 11) & 3) * 4 + ((cols >> 8) & 3)) * 256 + (rows & 255)) * 4
    lane_v[...] = cols & 127
    rmask = x * 2048 + c * 1024 + y * 256
    cmask = zh * 1024 + zl * 128
    bits = parity((rows & rmask) ^ (cols & cmask))
    sgn_v[...] = (1 - 2 * bits).astype(F32) * (1.0 / 8192)
    def index_a(i):
        return pltpu.make_async_copy(base_v.at[i], base_a, km.at[0])

    def index_b(i):
        return pltpu.make_async_copy(base_v.at[i], base_b, km.at[1])

    index_a(0).start()
    index_b(1).start()
    hm[...] = sylvester(256)

    def prepare():
        for q in range(4):
            got = remote(li, xq.at[q], xs_.at[0], xr.at[q], sibling)
            mine = (d == q) & (c == zh)
            seen = (c != zh) & ((q // 2) != zl)

            @pl.when(mine)
            def _():
                own_x.wait()

            @pl.when(jnp.logical_not(mine | seen))
            def _():
                got.wait_recv()

            @pl.when(d == q)
            def _():
                own_i.wait()

            @pl.when(d != q)
            def _():
                remote(ids, idall.at[q], ds_.at[0], dr.at[q], sibling).wait_recv()

        def labels(q):
            return jnp.concatenate([idall[q, i:i + 1, :] for i in range(4)], axis=1)

        big = idall[2, 0:1, 0:1]
        id0, id3 = labels(0), labels(3)
        short = id0 != big
        x0, x3 = xq[0].astype(F32).T, xq[3].astype(F32).T
        xtb[:, 0:512] = xq[1].astype(F32).T.astype(BF16)
        xtb[:, 512:1024] = xq[2].astype(F32).T.astype(BF16)
        xtb[:, 1024:1536] = jnp.where(short, x3, x0).astype(BF16)
        rest, id_rest = jnp.where(short, x0, x3), jnp.where(short, id0, id3)
        for o in range(3):
            label = o + (big <= o).astype(I32)
            xto[o * 256:(o + 1) * 256, :] = jnp.where(id_rest == label, rest, 0.0).astype(BF16)
        side = jnp.broadcast_to(short.astype(F32), (128, 512)).T.astype(BF16)
        mcol[...] = jnp.concatenate([side, side], axis=1)

    def pair(n):
        one, two = PAIRS[n]
        for u, v in (one, two):
            for piece in range(2):
                a, b = (-u) % 4, (-v) % 4
                qt = (zl if piece == 0 else 1 - zl) * 2 + 1 - c
                ref = gbuf.at[slot(u, v), qt]
                remote(ref, ref, ss.at[piece, a, b], sr.at[piece, a, b], sibling).wait_recv()
        sa, sb_ = slot(*one), slot(*two)

        @pl.when(c != zh)
        def _():
            for h, a in enumerate((sa, sb_)):
                remote(sgs.at[0], sg.at[a], sgss.at[0], sgr.at[n, h], sibling).wait_recv()

        w = [jnp.concatenate([gbuf[sa, q], gbuf[sb_, q]], axis=1) for q in range(4)]
        signs = jnp.concatenate([sg[sa], sg[sb_]], axis=1).astype(F32)
        short = mcol[...] != 0
        long_w = jnp.concatenate([w[1], w[2], jnp.where(short, w[3], w[0])], axis=0)
        g0 = jnp.dot(xtb[...], long_w, preferred_element_type=F32)
        g1 = jnp.dot(xto[...], jnp.where(short, w[0], w[3]), preferred_element_type=F32)
        for s in range(4):
            g = g0 if s == 0 else g1[(s - 1) * 256:s * 256]
            hi, lo = halves(g * signs)
            t = jnp.dot(hm[...], hi, preferred_element_type=F32) + jnp.dot(hm[...], lo, preferred_element_type=F32)
            zb[s, sa] = t[:, :128]
            zb[s, sb_] = t[:, 128:]

    own_g.wait()
    for op in OPS:
        if op == "signs":
            send_signs()
        elif op == "relay":
            relay()
        elif op == "inputs":
            prepare()
        elif isinstance(op, int):
            pair(op)
        else:
            arrived(*op)
            pass_on(*op)

    def fly(r, carry):
        for s in range(4):
            v = [zb[s, a, pl.ds(pl.multiple_of(r * 8, 8), 8), :] for a in range(16)]
            h = 1
            while h < 16:
                n = list(v)
                for a in range(16):
                    if a & h == 0:
                        n[a], n[a + h] = v[a] + v[a + h], v[a] - v[a + h]
                v = n
                h *= 2
            for a in range(16):
                z2[pl.ds(a * 1024 + r * 32 + s, 8, stride=4), :] = v[a]
        return carry

    lax.fori_loop(0, 32, fly, 0)

    stage = (sa0, sa1, sa2, sa3)
    lanes = lax.broadcasted_iota(I32, (8, 128), 1)
    sub = lax.broadcasted_iota(I32, (128, 128), 0)

    def fetch(t, base, n):
        for j in range(128):
            t[pl.ds(4 * j, 4), :] = z2[pl.ds(base[n, j], 4), :]

    def settle(ta, tb, i, n):
        h = jnp.concatenate(
            [jnp.where(parity(sub & lane_v[i, n + b:n + b + 1, :]) == 1, -1.0, 1.0).astype(BF16) for b in range(2)],
            axis=1,
        )
        both = [jnp.concatenate(halves(t[...]), axis=1) for t in (ta, tb)]
        r = jnp.dot(
            jnp.concatenate(both, axis=0), jnp.concatenate([h, h], axis=0), preferred_element_type=F32
        )
        for b in range(2):
            acc = [jnp.zeros((8, 128), F32) for _ in range(4)]
            for q in range(64):
                o = 512 * b + 8 * q
                acc[q % 4] = jnp.where((lanes >> 1) == q, r[o:o + 8, 128 * b:128 * b + 128], acc[q % 4])
            t = (acc[0] + acc[1]) + (acc[2] + acc[3])
            t = jnp.where((lanes[:4] & 1) == 0, t[:4], t[4:])
            for s in range(4):
                ps[s, i, n + b:n + b + 1, :] = t[s:s + 1, :]

    def pick(i, carry):
        for k, (index, base) in enumerate(((index_a, base_a), (index_b, base_b))):
            m = 2 * i + k
            index(m).wait()
            for n in range(4):
                fetch(stage[n], base, n)
            index(jnp.minimum(m + 2, 15)).start()
            settle(stage[0], stage[1], m, 0)
            settle(stage[2], stage[3], m, 2)
        return carry

    me8 = d * 2 + zh

    def emit(part):
        at = 8 * part
        big = jnp.broadcast_to(idall[2, 0:1, 0:1], (8, 4, 128))
        sign = sgn_v[at:at + 8]
        for e in range(4):
            t = jnp.where(big > e, ps[min(e + 1, 3), at:at + 8], ps[e, at:at + 8])
            t = jnp.where(big == e, ps[0, at:at + 8], t) * sign
            for h in range(2):
                for i in range(2):
                    pd[part, e * 2 + h, i, 0:4] = t[i * 4 + h * 2]
                    pd[part, e * 2 + h, i, 4:8] = t[i * 4 + h * 2 + 1]
        r1[part, me8] = pd[part, me8]
        for n, (k, m) in enumerate(line):
            tz, tc = (z + k) % 4, (c + m) % 2
            dest = ((tz % 2) * 2 + tc) * 2 + tz // 2
            cp = remote(pd.at[part, dest], r1.at[part, me8], s1.at[part, n], w1.at[part, me8], mate(k, m))
            cp.start()
            pending.append(cp)

    lax.fori_loop(0, 4, pick, 0)
    emit(0)
    lax.fori_loop(4, 8, pick, 0)
    emit(1)
    index_a(0).wait()
    index_b(0).wait()
    for part in range(2):
        for k, m in line:
            tz, tc = (z + k) % 4, (c + m) % 2
            src = ((tz % 2) * 2 + tc) * 2 + tz // 2
            remote(pd.at[part, src], r1.at[part, src], s1.at[part, 0], w1.at[part, src], sibling).wait_recv()
    for i in range(4):
        t = r1[i // 2, 0, i % 2]
        for n in range(1, 8):
            t = t + r1[i // 2, n, i % 2]
        for j in range(4):
            q2[i * 4 + j, 0:2, :] = t[2 * j:2 * j + 2, :]
            q2[i * 4 + j, 2:8, :] = jnp.zeros((6, 128), F32)
    r2[own] = q2[own]
    for n, (i, j) in enumerate(plane):
        dest = ((x + sig * i + 4) % 4) * 4 + (y + sig * j + 4) % 4
        cp = remote(q2.at[dest], r2.at[own], s2.at[n], w2.at[own], near(i, j))
        cp.start()
        pending.append(cp)
    for i, j in plane:
        src = ((x + sig * i + 4) % 4) * 4 + (y + sig * j + 4) % 4
        remote(q2.at[src], r2.at[src], s2.at[0], w2.at[src], sibling).wait_recv()
    t = r2[0]
    for n in range(1, 16):
        t = t + r2[n]
    out[...] = t

    @pl.when(c != zh)
    def _():
        near_x.wait_send()
        for cp in relays:
            cp.wait_send()

    x_side.wait_send()
    x_over.wait_send()
    for cp in pending:
        cp.wait_send()


def on_device(layer_input, output_grad, doc_ids, sign_bits, kept_rows, kept_cols):
    vm = pl.BlockSpec(memory_space=pltpu.VMEM)
    dma = pltpu.SemaphoreType.DMA
    scratch = [
        pltpu.VMEM((16, 4, 128), I32),
        pltpu.VMEM((16, 4, 128), I32),
        pltpu.VMEM((16, 4, 512, 128), BF16),
        pltpu.VMEM((4, 16, 256, 128), F32),
        pltpu.VMEM((16384, 128), F32),
        pltpu.VMEM((4, 512, 256), BF16),
        pltpu.VMEM((256, 1536), BF16),
        pltpu.VMEM((768, 512), BF16),
        pltpu.VMEM((16, 256, 128), BF16),
        pltpu.VMEM((16, 256, 128), I32),
        pltpu.VMEM((8, 256, 128), I32),
        pltpu.VMEM((8, 256, 128), BF16),
        pltpu.VMEM((4, 4, 128), I32),
        pltpu.VMEM((256, 256), BF16),
        pltpu.VMEM((512, 256), BF16),
        pltpu.VMEM((16, 4, 128), I32),
        pltpu.VMEM((16, 4, 128), I32),
        pltpu.VMEM((16, 4, 128), F32),
        pltpu.SMEM((4, 128), I32),
        pltpu.SMEM((4, 128), I32),
        pltpu.VMEM((512, 128), F32),
        pltpu.VMEM((512, 128), F32),
        pltpu.VMEM((512, 128), F32),
        pltpu.VMEM((512, 128), F32),
        pltpu.VMEM((4, 16, 4, 128), F32),
        pltpu.VMEM((2, 8, 2, 8, 128), F32),
        pltpu.VMEM((2, 8, 2, 8, 128), F32),
        pltpu.VMEM((16, 8, 128), F32),
        pltpu.VMEM((16, 8, 128), F32),
        dma((4,)), dma((31,)), dma((2, 4, 4)), dma((2, 4, 4)), dma((2, 4, 4)),
        dma((5,)), dma((4,)), dma(()), dma((3,)), dma((4,)),
        dma((8,)), dma((16,)), dma((8,)), dma((8, 2)), dma((2,)),
        dma((2, 7)), dma((2, 8)), dma((15,)), dma((16,)),
    ]
    got = pl.pallas_call(
        kernel,
        out_shape=jax.ShapeDtypeStruct((8, 128), F32),
        in_specs=[pl.BlockSpec(memory_space=pl.ANY)] * 6,
        out_specs=vm,
        scratch_shapes=scratch,
        compiler_params=pltpu.CompilerParams(
            collective_id=0, has_side_effects=True, vmem_limit_bytes=60 << 20
        ),
        name="sketch",
    )(
        layer_input, output_grad, doc_ids.reshape(4, 128), sign_bits,
        kept_rows.reshape(16, 4, 128), kept_cols.reshape(16, 4, 128),
    )
    return got[:2].reshape(1, 256)


def solution(mesh):
    placed = (P("doc", "param"), P("doc", "param"), P("doc"), P("param", None), P(), P())
    return jax.shard_map(
        on_device, mesh=mesh, in_specs=placed, out_specs=P("doc", "param"), check_vma=False
    )
```
